32 devices in a mesh: ax: 4 (over z), az: 8 (over y, x, core).
Axes of the slice: x: 2, y: 2, z: 4, core: 2. Of those that a mesh axis runs over, the one named last changes fastest.
Arguments:
- adjoint: float32 [3, 128, 512, 256], P(None, 'ax', 'az'), may hold values from -6 to 6
- primal: float32 [3, 128, 512, 256], P(None, 'ax', 'az'), may hold values from -6 to 6
- wall: int32 [128, 512], P('ax', 'az'), may hold values from 0 to 63
- owner: int32 [128, 512], P('ax', 'az'), may hold values from 0 to 1023, as said below
- adjacency: int32 [4, 256, 4], P('ax', 'az'), may hold values from 0 to 95
- counts: int32 [4, 256], P('ax', 'az'), may hold values from 32 to 128
- laplacian: float32 [4, 256, 128, 128], P('ax', 'az'), as said below
Outputs:
- adjoint_next: float32 [3, 128, 512, 256], P(None, 'ax', 'az')
- smoothed: float32 [4, 256, 128], P('ax', 'az')
The draws below stay inside these ranges and needn't reach their ends.
Inputs may be any that keep to these rules, and one draw needn't show every extreme that they name: `owner`: patch p lives on device p // 32 of the mesh in order ax then az. Among the columns of one device, at most 192 have owners on one device, and in every draw some owning devices receive exactly 192 from every device. `laplacian`: diagonal entries lie in 2 to 3, off-diagonal ones in -2 / 128 to 0.
All inputs are finite; a program needn't handle non-finite values.
Results may differ from the reference program's by a relative error of at most 0.0001.
Values sent between devices are 32-bit elements; how exact they have to be, the bound alone decides.
A program may use at most 128 MiB of HBM per device.

```python
import jax
import jax.numpy as jnp
from jax import lax

CX = 32
CA = 64
CR = 256
PV = 128
NP_DEV = 32
NEIGH = 4
SWEEPS = 3
NXG = 128
NAG = 512
PATCH_AZ = 256
N_AX = 4
N_AZ = 8


def draw_owner(key, part):
    devices_all = N_AX * N_AZ
    tiles_dev = CX * CA
    capacity = 3 * tiles_dev // devices_all
    slots_all = devices_all * capacity
    ranking = jax.random.permutation(jax.random.fold_in(key, 1), devices_all)
    heated = (ranking < devices_all // 4).astype(jnp.int32)

    def per_source(source_index):
        subkey = jax.random.fold_in(jax.random.fold_in(key, 7), source_index)
        slot_ids = jnp.arange(slots_all, dtype=jnp.int32)
        noise = jax.random.randint(jax.random.fold_in(subkey, 0), (slots_all,), 0, 4096)
        scores = (noise + heated[slot_ids // capacity] * 8192) * slots_all + slot_ids
        picked = lax.top_k(scores, tiles_dev)[1].astype(jnp.int32)
        target = picked // capacity
        shuffle = jax.random.permutation(jax.random.fold_in(subkey, 1), tiles_dev)
        target = target[shuffle]
        within = jax.random.randint(jax.random.fold_in(subkey, 2), (tiles_dev,), 0, NP_DEV)
        return target * NP_DEV + within
    owners = jax.vmap(per_source)(jnp.arange(devices_all, dtype=jnp.int32))
    owners = owners.reshape(N_AX, N_AZ, CX, CA).transpose(0, 2, 1, 3)
    return owners.reshape(N_AX * CX, N_AZ * CA).astype(jnp.int32)


def draw_laplacian(key, part):
    shape = (N_AX, NP_DEV * N_AZ, PV, PV)
    offdiag = -jax.random.uniform(jax.random.fold_in(key, 1), shape, jnp.float32, 0.0, 2.0 / PV)
    diagonal = 2.0 + jax.random.uniform(jax.random.fold_in(key, 2), shape[:3], jnp.float32)
    row_ids = lax.broadcasted_iota(jnp.int32, shape, 2)
    col_ids = lax.broadcasted_iota(jnp.int32, shape, 3)
    return jnp.where(row_ids == col_ids, diagonal[..., None], offdiag).astype(jnp.float32)


def with_ends(result, key, least, largest):
    index_at = [jax.random.randint(jax.random.fold_in(key, axis), (), 0, length) for axis, length in enumerate(result.shape)]
    longest = result.shape.index(max(result.shape))
    neighbour = index_at[:longest] + [(index_at[longest] + 1) % result.shape[longest]] + index_at[longest + 1:]
    return result.at[tuple(index_at)].set(least).at[tuple(neighbour)].set(largest)


def block_scale(rng, shape, split, least, largest):
    def one(position, parts):
        heights = jax.random.uniform(jax.random.fold_in(jax.random.fold_in(rng, 6), position), (parts,), jnp.float32, least / len(split), largest / len(split))
        return jnp.repeat(jnp.exp(heights), shape[position] // parts).reshape((-1,) + (1,) * (len(shape) - position - 1))

    loudness = one(*split[0])
    for cut in split[1:]:
        loudness = loudness * one(*cut)
    return loudness


def bell_draw(stream_key, shape, spread, reach, shards=(), kind=jnp.bfloat16):
    drawn = jax.random.normal(stream_key, shape, jnp.float32) * spread
    if len(shards) > 0:
        drawn = block_scale(stream_key, shape, shards, -0.22, 0.18) * drawn
    return jnp.clip(drawn, min=-reach, max=reach).astype(kind)


def setup_inputs(seed: int = 0) -> dict:
    streams_of = jax.random.split(jax.random.key(seed), 8)
    adjoint = bell_draw(streams_of[0], (3, NXG, NAG, CR), 1.0, 6.0, ((1, 4), (2, 8)), jnp.float32)
    primal = bell_draw(streams_of[1], (3, NXG, NAG, CR), 1.0, 6.0, ((1, 4), (2, 8)), jnp.float32)
    wall = with_ends(jax.random.randint(streams_of[2], (NXG, NAG), 0, CR // 4), jax.random.fold_in(streams_of[2], 1), 0, (CR // 4) - 1).astype(jnp.int32)
    owner = draw_owner(jax.random.fold_in(streams_of[7], 71), 0)
    adjacency = with_ends(jax.random.randint(streams_of[4], (N_AX, PATCH_AZ, NEIGH), 0, 3 * NP_DEV), jax.random.fold_in(streams_of[4], 1), 0, (3 * NP_DEV) - 1).astype(jnp.int32)
    counts = with_ends(jax.random.randint(streams_of[5], (N_AX, PATCH_AZ), PV // 4, PV + 1), jax.random.fold_in(streams_of[5], 1), PV // 4, PV).astype(jnp.int32)
    laplacian = draw_laplacian(jax.random.fold_in(streams_of[7], 71), 0)
    return {"adjoint": adjoint, "primal": primal, "wall": wall, "owner": owner, "adjacency": adjacency, "counts": counts, "laplacian": laplacian}


time_step = 0.12
viscosity = 1.0
wall_scale = 0.1
smoothing = 0.5
coupling = 0.25
relaxation = 0.25


def adjoint_update(masked, primal, fluid, x_plus, x_minus, a_plus, a_minus):
    radial = jnp.pad(masked, ((0, 0), (0, 0), (0, 0), (1, 1)))
    r_plus = radial[..., 2:]
    r_minus = radial[..., :-2]
    laplace = x_plus + x_minus + a_plus + a_minus + r_plus + r_minus - 6.0 * masked
    advect = primal[0][None] * (x_plus - x_minus) * 0.5
    advect = advect + primal[1][None] * (a_plus - a_minus) * 0.5
    advect = advect + primal[2][None] * (r_plus - r_minus) * 0.5
    return fluid[None] * (masked + time_step * (viscosity * laplace + advect))


def take_rows(field, index):
    return field[index]


def reference(adjoint, primal, wall, owner, adjacency, counts, laplacian):
    depth = lax.broadcasted_iota(jnp.int32, wall.shape + (CR,), 2)
    fluid = (depth >= wall[:, :, None]).astype(jnp.float32)
    masked = adjoint * fluid[None]
    padded = jnp.pad(masked, ((0, 0), (1, 1), (0, 0), (0, 0)))
    updated = adjoint_update(masked, primal, fluid, padded[:, 2:], padded[:, :-2],
                             jnp.roll(masked, -1, axis=2), jnp.roll(masked, 1, axis=2))
    tiles = jnp.sum(primal[..., :PV] * updated[..., :PV], axis=0)
    source = jax.ops.segment_sum(tiles.reshape(-1, PV), owner.reshape(-1),
                                 num_segments=N_AX * PATCH_AZ) * wall_scale
    source = source.reshape(N_AX, PATCH_AZ, PV)
    vertex = lax.broadcasted_iota(jnp.int32, (N_AX, PATCH_AZ, PV), 2)
    live = (vertex < counts[:, :, None]).astype(jnp.float32)
    rows = lax.broadcasted_iota(jnp.int32, adjacency.shape, 1)
    source_rows = ((rows // NP_DEV) * NP_DEV - NP_DEV + adjacency) % PATCH_AZ
    field = live * source
    for sweep in range(SWEEPS):
        gathered = jax.vmap(take_rows)(field, source_rows)
        neighbours = jnp.sum(gathered, axis=2)
        applied = jnp.einsum("ipvw,ipw->ipv", laplacian, field, precision=lax.Precision.HIGHEST)
        image = field + smoothing * (applied + coupling * (NEIGH * field - neighbours))
        field = live * (field + relaxation * (source - image))
    return updated, field
```

```python
import functools

import jax
import jax.numpy as jnp
from jax import lax
from jax.experimental import pallas as pl
from jax.experimental.pallas import tpu as pltpu
from jax.sharding import PartitionSpec as P

SWEEPS = 3

time_step = 0.12
viscosity = 1.0
wall_scale = 0.1
smoothing = 0.5
coupling = 0.25
relaxation = 0.25

F32 = jnp.float32
BF16 = jnp.bfloat16
MESH = pl.DeviceIdType.MESH
PAD = 8


def pieces(value):
    high = value.astype(BF16).astype(F32)
    return high, value - high


def column_of(row):
    n = row.shape[1]
    eye = lax.broadcasted_iota(jnp.int32, (n, n), 0) == lax.broadcasted_iota(jnp.int32, (n, n), 1)
    return jnp.sum(jnp.where(eye, jnp.broadcast_to(row, (n, n)), 0.0), axis=1, keepdims=True)


def stencil_kernel(
    planes, adjoint, primal, wall, x_low, x_high, a_low, a_high, out, tiles, held, depth_of, sems
):
    step = pl.program_id(0)
    axial, sector, radial = adjoint.shape[1:]
    vertices = tiles.shape[-1] // 2
    rows = 8

    def fetch(x):
        return pltpu.make_async_copy(
            adjoint.at[:, x], held.at[:, x + 1, pl.ds(PAD, sector), :], sems.at[x]
        )

    def mask_plane(x):
        fetch(x).wait()
        column = column_of(wall[pl.ds(x, 1), :].astype(F32))
        depth_of[x] = jnp.broadcast_to(column, (sector, radial))
        lane = lax.broadcasted_iota(jnp.int32, (sector, radial), 1).astype(F32)
        fluid = lane >= depth_of[x]
        for c in range(3):
            body = held[c, x + 1, PAD : PAD + sector, :]
            held[c, x + 1, PAD : PAD + sector, :] = jnp.where(fluid, body, 0.0)
            held[c, x + 1, PAD - 1 : PAD, :] = a_low[c, pl.ds(x, 1), :]
            held[c, x + 1, PAD + sector : PAD + sector + 1, :] = a_high[c, pl.ds(x, 1), :]

    @pl.when(step == 0)
    def _():
        def begin(x, carry):
            fetch(x).start()
            return carry

        lax.fori_loop(0, axial, begin, 0)
        for c in range(3):
            held[c, 0, PAD : PAD + sector, :] = x_low[c]
            held[c, axial + 1, PAD : PAD + sector, :] = x_high[c]
        mask_plane(0)

    lane = lax.broadcasted_iota(jnp.int32, (rows, radial), 1)
    first, last = lane == 0, lane == radial - 1
    lane_value = lane.astype(F32)

    def plane(j, carry):
        x = step * planes + j

        @pl.when(x + 1 < axial)
        def _():
            mask_plane(x + 1)

        for a in range(0, sector, rows):
            at = PAD + a
            fluid = lane_value >= depth_of[x, a : a + rows, :]
            flows = [primal[d, j, a : a + rows, :] for d in range(3)]
            half = [(0.5 * time_step) * flow for flow in flows]
            plus = [viscosity * time_step + value for value in half]
            minus = [viscosity * time_step - value for value in half]
            total = jnp.zeros((rows, vertices), F32)
            for c in range(3):
                middle = held[c, x + 1, at : at + rows, :]
                value = (1.0 - 6.0 * viscosity * time_step) * middle
                value += plus[0] * held[c, x + 2, at : at + rows, :]
                value += minus[0] * held[c, x, at : at + rows, :]
                value += plus[1] * held[c, x + 1, at + 1 : at + 1 + rows, :]
                value += minus[1] * held[c, x + 1, at - 1 : at - 1 + rows, :]
                value += plus[2] * jnp.where(last, 0.0, pltpu.roll(middle, radial - 1, 1))
                value += minus[2] * jnp.where(first, 0.0, pltpu.roll(middle, 1, 1))
                value = jnp.where(fluid, value, 0.0)
                out[c, j, a : a + rows, :] = value
                total += flows[c][:, :vertices] * value[:, :vertices]
            high, low = pieces(total)
            depth_of[x, a : a + rows, :vertices] = high
            depth_of[x, a : a + rows, vertices : 2 * vertices] = low
        tiles[j, 0] = depth_of[x, :, : 2 * vertices].astype(BF16)
        return carry

    lax.fori_loop(0, planes, plane, 0)


def stencil(adjoint, primal, wall, halos, vertices):
    comps, axial, sector, radial = adjoint.shape
    planes = 4
    steps = axial // planes
    vmem = pl.BlockSpec(memory_space=pltpu.VMEM)
    return pl.pallas_call(
        functools.partial(stencil_kernel, planes),
        grid=(steps,),
        out_shape=(
            jax.ShapeDtypeStruct(adjoint.shape, F32),
            jax.ShapeDtypeStruct((axial // 2, 2, sector, 2 * vertices), BF16),
        ),
        in_specs=[
            pl.BlockSpec(memory_space=pl.ANY),
            pl.BlockSpec((comps, planes, sector, radial), lambda i: (0, i, 0, 0)),
            vmem,
            vmem,
            vmem,
            vmem,
            vmem,
        ],
        out_specs=(
            pl.BlockSpec((comps, planes, sector, radial), lambda i: (0, i, 0, 0)),
            pl.BlockSpec(
                (planes, 1, sector, 2 * vertices),
                lambda i: (i % (steps // 2), i // (steps // 2), 0, 0),
            ),
        ),
        scratch_shapes=[
            pltpu.VMEM((comps, axial + 2, sector + 2 * PAD, radial), F32),
            pltpu.VMEM((axial, sector, radial), F32),
            pltpu.SemaphoreType.DMA((axial,)),
        ],
        compiler_params=pltpu.CompilerParams(vmem_limit_bytes=40 * 2**20),
        cost_estimate=pl.CostEstimate(
            flops=60 * adjoint.size, bytes_accessed=14 * adjoint.size, transcendentals=0
        ),
        name="stencil",
    )(adjoint, primal, wall, *halos)


def smooth_kernel(
    n_ax,
    n_az,
    tiles,
    owner,
    adjacency,
    counts,
    laplacian,
    out,
    matrices,
    matrix_pieces,
    pair_out,
    pair_own,
    pair_in,
    plane_sum,
    plane_in,
    axial_out,
    axial_in,
    ring_out,
    ring_in,
    matrix_sem,
    pair_sems,
    plane_sems,
    axial_sems,
    ring_sems,
):
    ax, az = lax.axis_index("ax"), lax.axis_index("az")
    patches, vertices = out.shape[1:]
    chips = n_az // 2
    chip, core = az // 2, az % 2
    sibling = chip * 2 + (1 - core)
    after, before = (az + 1) % n_az, (az + n_az - 1) % n_az
    half_rows = chips * patches

    load = pltpu.make_async_copy(laplacian.at[0], matrices, matrix_sem)
    load.start()

    barrier = pltpu.get_barrier_semaphore()
    partners = [(ax, sibling), (ax, after), (ax, before)]
    partners += [(ax, ((chip + d) % chips) * 2 + core) for d in range(1, chips)]
    partners += [((ax + d) % n_ax, az) for d in range(1, n_ax)]
    for partner in partners:
        pl.semaphore_signal(barrier, inc=1, device_id=partner, device_id_type=MESH)

    columns_half = owner.shape[0] // 2
    owners = jnp.concatenate([owner[:columns_half, :], owner[columns_half:, :]], axis=1)
    width = owners.shape[1]
    row = lax.broadcasted_iota(jnp.int32, (half_rows, width), 0)
    row_patch = (row // patches) * (2 * patches) + row % patches

    def partial_sum(target_ax, target_core):
        ids = row_patch + (target_ax * n_az + target_core) * patches
        hits = [
            jnp.where(ids == owners[b : b + 1, :], 1.0, 0.0).astype(BF16)
            for b in range(columns_half)
        ]
        both = jnp.dot(jnp.concatenate(hits, axis=1), tiles[...], preferred_element_type=F32)
        return both[:, :vertices] + both[:, vertices:]

    def remote(src, dst, sems, target):
        return pltpu.make_async_remote_copy(
            src_ref=src,
            dst_ref=dst,
            send_sem=sems.at[0],
            recv_sem=sems.at[1],
            device_id=target,
            device_id_type=MESH,
        )

    def pair_copy(t):
        return remote(pair_out.at[t], pair_in.at[t], pair_sems.at[t], (ax, sibling))

    def plane_copy(t, d):
        target = (chip + d) % chips
        return remote(
            plane_sum.at[t, target],
            plane_in.at[t, d - 1],
            plane_sems.at[t, d - 1],
            (ax, target * 2 + core),
        )

    def axial_copy(t):
        return remote(
            axial_out.at[t], axial_in.at[t], axial_sems.at[t], ((ax + 1 + t) % n_ax, az)
        )

    def plane_stage(t):
        pair_copy(t).wait()
        joined = pair_own[t] + pair_in[t]
        plane_sum[t] = joined.reshape(chips, patches, vertices)
        for d in range(1, chips):
            plane_copy(t, d).start()

    def axial_stage(t):
        for d in range(1, chips):
            plane_copy(t, d).wait()
        total = plane_sum[t, chip]
        for d in range(1, chips):
            total += plane_in[t, d - 1]
        axial_out[t] = total
        if t < n_ax - 1:
            axial_copy(t).start()

    for t in range(n_ax):
        target_ax = (ax + 1 + t) % n_ax
        pair_out[t] = partial_sum(target_ax, 1 - core)
        if t == 0:
            pl.semaphore_wait(barrier, len(partners))
        pair_copy(t).start()
        pair_own[t] = partial_sum(target_ax, core)
        if t >= 1:
            plane_stage(t - 1)
        if t >= 2:
            axial_stage(t - 2)
    plane_stage(n_ax - 1)
    axial_stage(n_ax - 2)

    load.wait()

    def split(p, carry):
        high, low = pieces(matrices[p])
        at = pl.multiple_of(p * vertices, vertices)
        matrix_pieces[pl.ds(at, vertices), :] = jnp.concatenate([high, low], axis=1).astype(BF16)
        return carry

    lax.fori_loop(0, patches, split, 0)

    vertex = lax.broadcasted_iota(jnp.int32, (patches, vertices), 1).astype(F32)
    live = vertex < column_of(counts[...].astype(F32))
    entries = adjacency[0]
    neighbours_each = entries.shape[1]
    index = lax.broadcasted_iota(jnp.int32, (patches, 3 * patches), 1)
    incidence = jnp.zeros((patches, 3 * patches), F32)
    for e in range(neighbours_each):
        incidence += jnp.where(index == entries[:, e : e + 1], 1.0, 0.0)
    incidence = incidence.astype(BF16)
    sub = lax.broadcasted_iota(jnp.int32, (8, vertices), 0)

    axial_stage(n_ax - 1)
    total = axial_out[n_ax - 1]
    for t in range(n_ax - 1):
        axial_copy(t).wait()
        total += axial_in[t]
    source = total * wall_scale

    def ring_copies(sweep):
        return (
            remote(ring_out.at[sweep], ring_in.at[sweep, 0], ring_sems.at[sweep, 0], (ax, after)),
            remote(ring_out.at[sweep], ring_in.at[sweep, 1], ring_sems.at[sweep, 1], (ax, before)),
        )

    field = jnp.where(live, source, 0.0)
    for sweep in range(SWEEPS):
        ring_out[sweep] = field
        for copy in ring_copies(sweep):
            copy.start()
        high, low = pieces(field)
        groups = []
        for g in range(0, patches, 8):
            stack = jnp.concatenate([high[g : g + 8], low[g : g + 8]], axis=0)
            stack = jnp.concatenate([stack, stack], axis=1).astype(BF16)
            products = lax.dot_general(
                stack,
                matrix_pieces[g * vertices : (g + 8) * vertices, :],
                (((1,), (1,)), ((), ())),
                preferred_element_type=F32,
            )
            products = products[:8] + products[8:]
            chosen = jnp.zeros((8, vertices), F32)
            for p in range(8):
                chosen = jnp.where(sub == p, products[:, p * vertices : (p + 1) * vertices], chosen)
            groups.append(chosen)
        applied = jnp.concatenate(groups, axis=0)
        for copy in ring_copies(sweep):
            copy.wait()
        around = jnp.concatenate([ring_in[sweep, 0], field, ring_in[sweep, 1]], axis=0)
        around = jnp.concatenate(pieces(around), axis=1).astype(BF16)
        near = jnp.dot(incidence, around, preferred_element_type=F32)
        near = near[:, :vertices] + near[:, vertices:]
        image = field + smoothing * (applied + coupling * (neighbours_each * field - near))
        field = jnp.where(live, field + relaxation * (source - image), 0.0)
    out[0] = field


def smooth(tiles, owner, adjacency, counts, laplacian):
    n_ax, n_az = lax.axis_size("ax"), lax.axis_size("az")
    patches, vertices = laplacian.shape[1:3]
    chips = n_az // 2
    block = (patches, vertices)
    half = (chips * patches, vertices)
    vmem = pl.BlockSpec(memory_space=pltpu.VMEM)
    dma = pltpu.SemaphoreType.DMA
    return pl.pallas_call(
        functools.partial(smooth_kernel, n_ax, n_az),
        out_shape=jax.ShapeDtypeStruct((1,) + block, F32),
        in_specs=[vmem, vmem, vmem, vmem, pl.BlockSpec(memory_space=pl.ANY)],
        out_specs=vmem,
        scratch_shapes=[
            pltpu.VMEM(laplacian.shape[1:], F32),
            pltpu.VMEM((patches * vertices, 2 * vertices), BF16),
            pltpu.VMEM((n_ax,) + half, F32),
            pltpu.VMEM((n_ax,) + half, F32),
            pltpu.VMEM((n_ax,) + half, F32),
            pltpu.VMEM((n_ax, chips) + block, F32),
            pltpu.VMEM((n_ax, chips - 1) + block, F32),
            pltpu.VMEM((n_ax,) + block, F32),
            pltpu.VMEM((n_ax,) + block, F32),
            pltpu.VMEM((SWEEPS,) + block, F32),
            pltpu.VMEM((SWEEPS, 2) + block, F32),
            dma,
            dma((n_ax, 2)),
            dma((n_ax, chips - 1, 2)),
            dma((n_ax, 2)),
            dma((SWEEPS, 2, 2)),
        ],
        compiler_params=pltpu.CompilerParams(
            collective_id=0, has_side_effects=True, vmem_limit_bytes=40 * 2**20
        ),
        name="smooth",
    )(tiles, owner, adjacency, counts, laplacian)


def exchange(last, first, axis, periodic):
    count = lax.axis_size(axis)
    forward = [(i, i + 1) for i in range(count - 1)]
    if periodic:
        forward.append((count - 1, 0))
    backward = [(target, source) for source, target in forward]
    return lax.ppermute(last, axis, forward), lax.ppermute(first, axis, backward)


def shards(adjoint, primal, wall, owner, adjacency, counts, laplacian):
    radial = adjoint.shape[3]
    vertices = laplacian.shape[2]

    def kept(layer, depths):
        lane = lax.broadcasted_iota(jnp.int32, depths.shape + (radial,), 1)
        return jnp.where((lane >= depths[:, None])[None], layer, 0.0)

    x_halos = exchange(
        kept(adjoint[:, -1], wall[-1]), kept(adjoint[:, 0], wall[0]), "ax", False
    )
    a_halos = exchange(
        kept(adjoint[:, :, -1], wall[:, -1]), kept(adjoint[:, :, 0], wall[:, 0]), "az", True
    )
    updated, tiles = stencil(adjoint, primal, wall, x_halos + a_halos, vertices)
    tiles = tiles.reshape(-1, 2 * vertices)
    return updated, smooth(tiles, owner, adjacency, counts, laplacian)


def solution(mesh):
    in_specs = (
        P(None, "ax", "az", None),
        P(None, "ax", "az", None),
        P("ax", "az"),
        P("ax", "az"),
        P("ax", "az", None),
        P("ax", "az"),
        P("ax", "az", None, None),
    )
    out_specs = (P(None, "ax", "az", None), P("ax", "az", None))
    return jax.shard_map(shards, mesh=mesh, in_specs=in_specs, out_specs=out_specs, check_vma=False)
```

```python
import functools

import jax
import jax.numpy as jnp
from jax import lax
from jax.experimental import pallas as pl
from jax.experimental.pallas import tpu as pltpu
from jax.sharding import PartitionSpec as P

SWEEPS = 3

time_step = 0.12
viscosity = 1.0
wall_scale = 0.1
smoothing = 0.5
coupling = 0.25
relaxation = 0.25

F32 = jnp.float32
BF16 = jnp.bfloat16
MESH = pl.DeviceIdType.MESH
PAD = 8


def pieces(value):
    high = value.astype(BF16).astype(F32)
    return high, value - high


def column_of(row):
    n = row.shape[1]
    eye = lax.broadcasted_iota(jnp.int32, (n, n), 0) == lax.broadcasted_iota(jnp.int32, (n, n), 1)
    return jnp.sum(jnp.where(eye, jnp.broadcast_to(row, (n, n)), 0.0), axis=1, keepdims=True)


def stencil_kernel(
    planes, adjoint, primal, wall, x_low, x_high, a_low, a_high, out, tiles, held, depth_of, sems
):
    step = pl.program_id(0)
    axial, sector, radial = adjoint.shape[1:]
    vertices = tiles.shape[-1] // 2
    rows = 8

    def fetch(x):
        return pltpu.make_async_copy(
            adjoint.at[:, x], held.at[:, x + 1, pl.ds(PAD, sector), :], sems.at[x]
        )

    full_lane = lax.broadcasted_iota(jnp.int32, (sector, radial), 1).astype(F32)

    def mask_plane(x):
        fetch(x).wait()
        depth = depth_of[x]
        fluid = full_lane >= jnp.concatenate([depth] * (radial // depth.shape[1]), axis=1)
        for c in range(3):
            body = held[c, x + 1, PAD : PAD + sector, :]
            held[c, x + 1, PAD : PAD + sector, :] = jnp.where(fluid, body, 0.0)
            held[c, x + 1, PAD - 1 : PAD, :] = a_low[c, pl.ds(x, 1), :]
            held[c, x + 1, PAD + sector : PAD + sector + 1, :] = a_high[c, pl.ds(x, 1), :]

    @pl.when(step == 0)
    def _():
        def begin(x, carry):
            fetch(x).start()
            return carry

        lax.fori_loop(0, axial, begin, 0)
        for c in range(3):
            held[c, 0, PAD : PAD + sector, :] = x_low[c]
            held[c, axial + 1, PAD : PAD + sector, :] = x_high[c]
        depths = wall[...].astype(F32)
        for x in range(axial):
            column = column_of(depths[x : x + 1, :])
            depth_of[x] = jnp.broadcast_to(column, depth_of.shape[1:])
        mask_plane(0)

    for j in range(1, planes):
        mask_plane(step * planes + j)

    @pl.when(step * planes + planes < axial)
    def _():
        mask_plane(step * planes + planes)

    lane = lax.broadcasted_iota(jnp.int32, (rows, radial), 1)
    sub = lax.broadcasted_iota(jnp.int32, (rows, radial), 0)
    first, last = lane == 0, lane == radial - 1
    top, bottom = sub == 0, sub == rows - 1
    lane_value = lane.astype(F32)

    def plane(j, carry):
        x = step * planes + j

        def block(c, at):
            return held[c, x + 1, at : at + rows, :]

        middles = [block(c, PAD) for c in range(3)]
        downs = [pltpu.roll(block(c, PAD - rows), 1, 0) for c in range(3)]
        ups = [pltpu.roll(middles[c], rows - 1, 0) for c in range(3)]
        highs, lows = [], []
        for a in range(0, sector, rows):
            at = PAD + a
            depth = depth_of[x, a : a + rows, :]
            fluid = lane_value >= jnp.concatenate([depth] * (radial // depth.shape[1]), axis=1)
            flows = [primal[d, j, a : a + rows, :] for d in range(3)]
            half = [(0.5 * time_step) * flow for flow in flows]
            plus = [viscosity * time_step + value for value in half]
            minus = [viscosity * time_step - value for value in half]
            plus[2] = jnp.where(last, 0.0, plus[2])
            minus[2] = jnp.where(first, 0.0, minus[2])
            total = jnp.zeros((rows, vertices), F32)
            for c in range(3):
                middle = middles[c]
                follow = block(c, at + rows)
                down = pltpu.roll(middle, 1, 0)
                up = pltpu.roll(follow, rows - 1, 0)
                value = (1.0 - 6.0 * viscosity * time_step) * middle
                value += plus[0] * held[c, x + 2, at : at + rows, :]
                value += minus[0] * held[c, x, at : at + rows, :]
                value += plus[1] * jnp.where(bottom, up, ups[c])
                value += minus[1] * jnp.where(top, downs[c], down)
                value += plus[2] * pltpu.roll(middle, radial - 1, 1)
                value += minus[2] * pltpu.roll(middle, 1, 1)
                value = jnp.where(fluid, value, 0.0)
                out[c, j, a : a + rows, :] = value
                total += flows[c][:, :vertices] * value[:, :vertices]
                middles[c], downs[c], ups[c] = follow, down, up
            high, low = pieces(total)
            highs.append(high)
            lows.append(low)
        both = [jnp.concatenate(part, axis=0) for part in (highs, lows)]
        tiles[j, 0] = jnp.concatenate(both, axis=1).astype(BF16)
        return carry

    lax.fori_loop(0, planes, plane, 0)


def stencil(adjoint, primal, wall, halos, vertices):
    comps, axial, sector, radial = adjoint.shape
    planes = 4
    steps = axial // planes
    vmem = pl.BlockSpec(memory_space=pltpu.VMEM)
    return pl.pallas_call(
        functools.partial(stencil_kernel, planes),
        grid=(steps,),
        out_shape=(
            jax.ShapeDtypeStruct(adjoint.shape, F32),
            jax.ShapeDtypeStruct((axial // 2, 2, sector, 2 * vertices), BF16),
        ),
        in_specs=[
            pl.BlockSpec(memory_space=pl.ANY),
            pl.BlockSpec((comps, planes, sector, radial), lambda i: (0, i, 0, 0)),
            vmem,
            vmem,
            vmem,
            vmem,
            vmem,
        ],
        out_specs=(
            pl.BlockSpec((comps, planes, sector, radial), lambda i: (0, i, 0, 0)),
            pl.BlockSpec(
                (planes, 1, sector, 2 * vertices),
                lambda i: (i % (steps // 2), i // (steps // 2), 0, 0),
            ),
        ),
        scratch_shapes=[
            pltpu.VMEM((comps, axial + 2, sector + 2 * PAD, radial), F32),
            pltpu.VMEM((axial, sector, vertices), F32),
            pltpu.SemaphoreType.DMA((axial,)),
        ],
        compiler_params=pltpu.CompilerParams(vmem_limit_bytes=60 * 2**20),
        cost_estimate=pl.CostEstimate(
            flops=60 * adjoint.size, bytes_accessed=14 * adjoint.size, transcendentals=0
        ),
        name="stencil",
    )(adjoint, primal, wall, *halos)


def smooth_kernel(
    n_ax,
    n_az,
    tiles,
    owner,
    adjacency,
    counts,
    laplacian,
    out,
    matrices,
    pair_out,
    pair_own,
    pair_in,
    plane_sum,
    plane_in,
    axial_out,
    axial_in,
    ring_out,
    ring_in,
    matrix_sem,
    pair_sems,
    plane_sems,
    axial_sems,
    ring_sems,
):
    ax, az = lax.axis_index("ax"), lax.axis_index("az")
    patches, vertices = out.shape[1:]
    chips = n_az // 2
    chip, core = az // 2, az % 2
    sibling = chip * 2 + (1 - core)
    after, before = (az + 1) % n_az, (az + n_az - 1) % n_az
    half_rows = chips * patches

    load = pltpu.make_async_copy(laplacian, matrices, matrix_sem)
    load.start()

    barrier = pltpu.get_barrier_semaphore()
    partners = [(ax, sibling), (ax, after), (ax, before)]
    partners += [(ax, ((chip + d) % chips) * 2 + core) for d in range(1, chips)]
    partners += [((ax + d) % n_ax, az) for d in range(1, n_ax)]
    for partner in partners:
        pl.semaphore_signal(barrier, inc=1, device_id=partner, device_id_type=MESH)

    columns_half = owner.shape[0] // 2
    owners = jnp.concatenate([owner[:columns_half, :], owner[columns_half:, :]], axis=1)
    width = owners.shape[1]
    row = lax.broadcasted_iota(jnp.int32, (2 * half_rows, width), 0)
    row_core = jnp.where(row < half_rows, 1 - core, core)
    row_chip = (row % half_rows) // patches
    row_patch = (row_chip * 2 + row_core) * patches + row % patches

    def partial_sum(target_ax):
        ids = row_patch + target_ax * n_az * patches
        hits = [
            jnp.where(ids == owners[b : b + 1, :], 1.0, 0.0).astype(BF16)
            for b in range(columns_half)
        ]
        both = jnp.dot(jnp.concatenate(hits, axis=1), tiles[...], preferred_element_type=F32)
        return both[:, :vertices] + both[:, vertices:]

    def remote(src, dst, sems, target):
        return pltpu.make_async_remote_copy(
            src_ref=src,
            dst_ref=dst,
            send_sem=sems.at[0],
            recv_sem=sems.at[1],
            device_id=target,
            device_id_type=MESH,
        )

    def pair_copy(t):
        return remote(pair_out.at[t], pair_in.at[t], pair_sems.at[t], (ax, sibling))

    def plane_copy(t, d):
        target = (chip + d) % chips
        return remote(
            plane_sum.at[t, target],
            plane_in.at[t, d - 1],
            plane_sems.at[t, d - 1],
            (ax, target * 2 + core),
        )

    def axial_copy(t):
        return remote(
            axial_out.at[t], axial_in.at[t], axial_sems.at[t], ((ax + 1 + t) % n_ax, az)
        )

    def plane_stage(t):
        pair_copy(t).wait()
        joined = pair_own[t] + pair_in[t]
        plane_sum[t] = joined.reshape(chips, patches, vertices)
        for d in range(1, chips):
            plane_copy(t, d).start()

    def axial_stage(t):
        for d in range(1, chips):
            plane_copy(t, d).wait()
        total = plane_sum[t, chip]
        for d in range(1, chips):
            total += plane_in[t, d - 1]
        axial_out[t] = total
        if t < n_ax - 1:
            axial_copy(t).start()

    for t in range(n_ax):
        target_ax = (ax + 1 + t) % n_ax
        partial = partial_sum(target_ax)
        pair_out[t] = partial[:half_rows]
        pair_own[t] = partial[half_rows:]
        if t == 0:
            pl.semaphore_wait(barrier, len(partners))
        pair_copy(t).start()
        if t >= 1:
            plane_stage(t - 1)
        if t >= 2:
            axial_stage(t - 2)
    plane_stage(n_ax - 1)
    axial_stage(n_ax - 2)

    load.wait()
    vertex = lax.broadcasted_iota(jnp.int32, (patches, vertices), 1).astype(F32)
    live = vertex < column_of(counts[...].astype(F32))
    entries = adjacency[0]
    neighbours_each = entries.shape[1]
    index = lax.broadcasted_iota(jnp.int32, (patches, 3 * patches), 1)
    incidence = jnp.zeros((patches, 3 * patches), F32)
    for e in range(neighbours_each):
        incidence += jnp.where(index == entries[:, e : e + 1], 1.0, 0.0)
    incidence = incidence.astype(BF16)
    sub = lax.broadcasted_iota(jnp.int32, (8, vertices), 0)

    axial_stage(n_ax - 1)
    total = axial_out[n_ax - 1]
    for t in range(n_ax - 1):
        axial_copy(t).wait()
        total += axial_in[t]
    source = total * wall_scale

    def ring_copies(sweep):
        return (
            remote(ring_out.at[sweep], ring_in.at[sweep, 0], ring_sems.at[sweep, 0], (ax, after)),
            remote(ring_out.at[sweep], ring_in.at[sweep, 1], ring_sems.at[sweep, 1], (ax, before)),
        )

    field = jnp.where(live, source, 0.0)
    for sweep in range(SWEEPS):
        ring_out[sweep] = field
        for copy in ring_copies(sweep):
            copy.start()
        high, low = pieces(field)
        groups = []
        for g in range(0, patches, 8):
            stack = jnp.concatenate([high[g : g + 8], low[g : g + 8]], axis=0)
            stack = jnp.concatenate([stack, stack], axis=1).astype(BF16)
            products = jnp.dot(
                stack,
                matrices[:, g * vertices : (g + 8) * vertices],
                preferred_element_type=F32,
            )
            products = products[:8] + products[8:]
            chosen = jnp.zeros((8, vertices), F32)
            for p in range(8):
                chosen = jnp.where(sub == p, products[:, p * vertices : (p + 1) * vertices], chosen)
            groups.append(chosen)
        applied = jnp.concatenate(groups, axis=0)
        for copy in ring_copies(sweep):
            copy.wait()
        around = jnp.concatenate([ring_in[sweep, 0], field, ring_in[sweep, 1]], axis=0)
        around = jnp.concatenate(pieces(around), axis=1).astype(BF16)
        near = jnp.dot(incidence, around, preferred_element_type=F32)
        near = near[:, :vertices] + near[:, vertices:]
        image = field + smoothing * (applied + coupling * (neighbours_each * field - near))
        field = jnp.where(live, field + relaxation * (source - image), 0.0)
    out[0] = field


def smooth(tiles, owner, adjacency, counts, laplacian, vertices):
    n_ax, n_az = lax.axis_size("ax"), lax.axis_size("az")
    patches = laplacian.shape[1] // vertices
    chips = n_az // 2
    block = (patches, vertices)
    half = (chips * patches, vertices)
    vmem = pl.BlockSpec(memory_space=pltpu.VMEM)
    dma = pltpu.SemaphoreType.DMA
    return pl.pallas_call(
        functools.partial(smooth_kernel, n_ax, n_az),
        out_shape=jax.ShapeDtypeStruct((1,) + block, F32),
        in_specs=[vmem, vmem, vmem, vmem, pl.BlockSpec(memory_space=pl.ANY)],
        out_specs=vmem,
        scratch_shapes=[
            pltpu.VMEM(laplacian.shape, BF16),
            pltpu.VMEM((n_ax,) + half, F32),
            pltpu.VMEM((n_ax,) + half, F32),
            pltpu.VMEM((n_ax,) + half, F32),
            pltpu.VMEM((n_ax, chips) + block, F32),
            pltpu.VMEM((n_ax, chips - 1) + block, F32),
            pltpu.VMEM((n_ax,) + block, F32),
            pltpu.VMEM((n_ax,) + block, F32),
            pltpu.VMEM((SWEEPS,) + block, F32),
            pltpu.VMEM((SWEEPS, 2) + block, F32),
            dma,
            dma((n_ax, 2)),
            dma((n_ax, chips - 1, 2)),
            dma((n_ax, 2)),
            dma((SWEEPS, 2, 2)),
        ],
        compiler_params=pltpu.CompilerParams(
            collective_id=0, has_side_effects=True, vmem_limit_bytes=40 * 2**20
        ),
        name="smooth",
    )(tiles, owner, adjacency, counts, laplacian)


def halo_kernel(
    n_ax,
    n_az,
    adjoint,
    wall,
    laplacian,
    x_low,
    x_high,
    a_low,
    a_high,
    pieces_out,
    x_in,
    a_in,
    x_wall,
    a_wall,
    matrices,
    matrix_sem,
    x_sems,
    a_sems,
):
    ax, az = lax.axis_index("ax"), lax.axis_index("az")
    axial, sector, radial = adjoint.shape[1:]
    patches, vertices = laplacian.shape[1:3]
    above, below = ((ax + 1) % n_ax, az), ((ax + n_ax - 1) % n_ax, az)
    after, before = (ax, (az + 1) % n_az), (ax, (az + n_az - 1) % n_az)

    load = pltpu.make_async_copy(laplacian.at[0], matrices, matrix_sem)
    barrier = pltpu.get_barrier_semaphore()
    for partner in (above, below, after, before):
        pl.semaphore_signal(barrier, inc=1, device_id=partner, device_id_type=MESH)
    pl.semaphore_wait(barrier, 4)

    def remote(src, dst, sems, target):
        return pltpu.make_async_remote_copy(
            src_ref=src,
            dst_ref=dst,
            send_sem=sems.at[0],
            recv_sem=sems.at[1],
            device_id=target,
            device_id_type=MESH,
        )

    def x_copies(side):
        layer = adjoint.at[:, axial - 1] if side == 0 else adjoint.at[:, 0]
        target = above if side == 0 else below
        return (
            remote(layer, x_in.at[side], x_sems.at[side, 0], target),
            remote(wall, x_wall.at[side], x_sems.at[side, 1], target),
        )

    def a_copies(side):
        layer = adjoint.at[:, :, sector - 1] if side == 0 else adjoint.at[:, :, 0]
        target = after if side == 0 else before
        return (
            remote(layer, a_in.at[side], a_sems.at[side, 0], target),
            remote(wall, a_wall.at[side], a_sems.at[side, 1], target),
        )

    sends = (ax < n_ax - 1, ax > 0)
    takes = (ax > 0, ax < n_ax - 1)
    for side in range(2):

        @pl.when(sends[side])
        def _():
            for copy in x_copies(side):
                copy.start()

    for side in range(2):
        for copy in a_copies(side):
            copy.start()

    load.start()
    load.wait()

    def split(p, carry):
        high, low = pieces(matrices[p].T)
        at = pl.multiple_of(p * vertices, vertices)
        pieces_out[:vertices, pl.ds(at, vertices)] = high.astype(BF16)
        pieces_out[vertices:, pl.ds(at, vertices)] = low.astype(BF16)
        return carry

    lax.fori_loop(0, patches, split, 0, unroll=4)

    lane = lax.broadcasted_iota(jnp.int32, (axial, radial), 1)
    for side, (target, at) in enumerate(((a_low, sector - 1), (a_high, 0))):
        for copy in a_copies(side):
            copy.wait()
        fluid = lane >= a_wall[side][:, at : at + 1]
        for c in range(3):
            target[c] = jnp.where(fluid, a_in[side, c], 0.0)

    lane = lax.broadcasted_iota(jnp.int32, (sector, radial), 1).astype(F32)
    for side, (target, at) in enumerate(((x_low, axial - 1), (x_high, 0))):

        @pl.when(sends[side])
        def _():
            for copy in x_copies(side):
                copy.wait_send()

        @pl.when(takes[side])
        def _():
            for copy in x_copies(side):
                copy.wait_recv()
            fluid = lane >= column_of(x_wall[side][at : at + 1, :].astype(F32))
            for c in range(3):
                target[c] = jnp.where(fluid, x_in[side, c], 0.0)

        @pl.when(jnp.logical_not(takes[side]))
        def _():
            target[...] = jnp.zeros(target.shape, F32)


def halos(adjoint, wall, laplacian):
    n_ax, n_az = lax.axis_size("ax"), lax.axis_size("az")
    comps, axial, sector, radial = adjoint.shape
    patches, vertices = laplacian.shape[1:3]
    vmem = pl.BlockSpec(memory_space=pltpu.VMEM)
    anywhere = pl.BlockSpec(memory_space=pl.ANY)
    dma = pltpu.SemaphoreType.DMA
    x_layer = (comps, sector, radial)
    a_layer = (comps, axial, radial)
    return pl.pallas_call(
        functools.partial(halo_kernel, n_ax, n_az),
        out_shape=(
            jax.ShapeDtypeStruct(x_layer, F32),
            jax.ShapeDtypeStruct(x_layer, F32),
            jax.ShapeDtypeStruct(a_layer, F32),
            jax.ShapeDtypeStruct(a_layer, F32),
            jax.ShapeDtypeStruct((2 * vertices, patches * vertices), BF16),
        ),
        in_specs=[anywhere, vmem, anywhere],
        out_specs=(vmem,) * 5,
        scratch_shapes=[
            pltpu.VMEM((2,) + x_layer, F32),
            pltpu.VMEM((2,) + a_layer, F32),
            pltpu.VMEM((2,) + wall.shape, jnp.int32),
            pltpu.VMEM((2,) + wall.shape, jnp.int32),
            pltpu.VMEM(laplacian.shape[1:], F32),
            dma,
            dma((2, 2, 2)),
            dma((2, 2, 2)),
        ],
        compiler_params=pltpu.CompilerParams(
            collective_id=1, has_side_effects=True, vmem_limit_bytes=60 * 2**20
        ),
        name="halos",
    )(adjoint, wall, laplacian)


def shards(adjoint, primal, wall, owner, adjacency, counts, laplacian):
    vertices = laplacian.shape[2]
    *layers, matrices = halos(adjoint, wall, laplacian)
    updated, tiles = stencil(adjoint, primal, wall, layers, vertices)
    tiles = tiles.reshape(-1, 2 * vertices)
    return updated, smooth(tiles, owner, adjacency, counts, matrices, vertices)


def solution(mesh):
    in_specs = (
        P(None, "ax", "az", None),
        P(None, "ax", "az", None),
        P("ax", "az"),
        P("ax", "az"),
        P("ax", "az", None),
        P("ax", "az"),
        P("ax", "az", None, None),
    )
    out_specs = (P(None, "ax", "az", None), P("ax", "az", None))
    return jax.shard_map(shards, mesh=mesh, in_specs=in_specs, out_specs=out_specs, check_vma=False)
```

```python
import functools

import jax
import jax.numpy as jnp
from jax import lax
from jax.experimental import pallas as pl
from jax.experimental.pallas import tpu as pltpu
from jax.sharding import PartitionSpec as P

SWEEPS = 3

time_step = 0.12
viscosity = 1.0
wall_scale = 0.1
smoothing = 0.5
coupling = 0.25
relaxation = 0.25

F32 = jnp.float32
BF16 = jnp.bfloat16
MESH = pl.DeviceIdType.MESH
PAD = 8


def pieces(value):
    high = value.astype(BF16).astype(F32)
    return high, value - high


def column_of(row):
    n = row.shape[1]
    eye = lax.broadcasted_iota(jnp.int32, (n, n), 0) == lax.broadcasted_iota(jnp.int32, (n, n), 1)
    return jnp.sum(jnp.where(eye, jnp.broadcast_to(row, (n, n)), 0.0), axis=1, keepdims=True)


def stencil_kernel(
    planes, adjoint, primal, wall, x_low, x_high, a_low, a_high, out, tiles, held, depth_of, sems
):
    step = pl.program_id(0)
    axial, sector, radial = adjoint.shape[1:]
    vertices = tiles.shape[-1] // 2
    rows = 8

    def fetch(x):
        return pltpu.make_async_copy(
            adjoint.at[:, x], held.at[:, x + 1, pl.ds(PAD, sector), :], sems.at[x]
        )

    def side_rows(x):
        for c in range(3):
            held[c, x + 1, PAD - 1 : PAD, :] = a_low[c, pl.ds(x, 1), :]
            held[c, x + 1, PAD + sector : PAD + sector + 1, :] = a_high[c, pl.ds(x, 1), :]

    @pl.when(step == 0)
    def _():
        def begin(x, carry):
            fetch(x).start()
            return carry

        lax.fori_loop(0, axial, begin, 0)
        for c in range(3):
            held[c, 0, PAD : PAD + sector, :] = x_low[c]
            held[c, axial + 1, PAD : PAD + sector, :] = x_high[c]
        depths = wall[...].astype(F32)
        for x in range(axial):
            column = column_of(depths[x : x + 1, :])
            depth_of[x] = jnp.broadcast_to(column, depth_of.shape[1:])
        depth_of[axial] = jnp.zeros(depth_of.shape[1:], F32)
        fetch(0).wait()
        side_rows(0)
        full_lane = lax.broadcasted_iota(jnp.int32, (sector, radial), 1).astype(F32)
        solid = full_lane < jnp.concatenate([depth_of[0]] * (radial // vertices), axis=1)
        for c in range(3):
            body = held[c, 1, PAD : PAD + sector, :]
            held[c, 1, PAD : PAD + sector, :] = jnp.where(solid, 0.0, body)

    lane = lax.broadcasted_iota(jnp.int32, (rows, radial), 1)
    sub = lax.broadcasted_iota(jnp.int32, (rows, radial), 0)
    first, last = lane == 0, lane == radial - 1
    top, bottom = sub == 0, sub == rows - 1
    lane_value = lane.astype(F32)

    def plane(j, carry):
        x = step * planes + j

        @pl.when(x + 1 < axial)
        def _():
            fetch(x + 1).wait()
            side_rows(x + 1)

        def fluid_at(x, a):
            depth = depth_of[x, a : a + rows, :]
            return lane_value >= jnp.concatenate([depth] * (radial // vertices), axis=1)

        def block(c, at):
            return held[c, x + 1, at : at + rows, :]

        middles = [block(c, PAD) for c in range(3)]
        downs = [pltpu.roll(block(c, PAD - rows), 1, 0) for c in range(3)]
        ups = [pltpu.roll(middles[c], rows - 1, 0) for c in range(3)]
        highs, lows = [], []
        for a in range(0, sector, rows):
            at = PAD + a
            fluid, fluid_next = fluid_at(x, a), fluid_at(x + 1, a)
            flows = [primal[d, j, a : a + rows, :] for d in range(3)]
            half = [(0.5 * time_step) * flow for flow in flows]
            plus = [viscosity * time_step + value for value in half]
            minus = [viscosity * time_step - value for value in half]
            plus[2] = jnp.where(last, 0.0, plus[2])
            minus[2] = jnp.where(first, 0.0, minus[2])
            total = jnp.zeros((rows, vertices), F32)
            for c in range(3):
                middle = middles[c]
                follow = block(c, at + rows)
                down = pltpu.roll(middle, 1, 0)
                up = pltpu.roll(follow, rows - 1, 0)
                value = (1.0 - 6.0 * viscosity * time_step) * middle
                ahead = jnp.where(fluid_next, held[c, x + 2, at : at + rows, :], 0.0)
                held[c, x + 2, at : at + rows, :] = ahead
                value += plus[0] * ahead
                value += minus[0] * held[c, x, at : at + rows, :]
                value += plus[1] * jnp.where(bottom, up, ups[c])
                value += minus[1] * jnp.where(top, downs[c], down)
                value += plus[2] * pltpu.roll(middle, radial - 1, 1)
                value += minus[2] * pltpu.roll(middle, 1, 1)
                value = jnp.where(fluid, value, 0.0)
                out[c, j, a : a + rows, :] = value
                total += flows[c][:, :vertices] * value[:, :vertices]
                middles[c], downs[c], ups[c] = follow, down, up
            high, low = pieces(total)
            highs.append(high)
            lows.append(low)
        both = [jnp.concatenate(part, axis=0) for part in (highs, lows)]
        tiles[j, 0] = jnp.concatenate(both, axis=1).astype(BF16)
        return carry

    lax.fori_loop(0, planes, plane, 0)


def stencil(adjoint, primal, wall, halos, vertices):
    comps, axial, sector, radial = adjoint.shape
    planes = 4
    steps = axial // planes
    vmem = pl.BlockSpec(memory_space=pltpu.VMEM)
    return pl.pallas_call(
        functools.partial(stencil_kernel, planes),
        grid=(steps,),
        out_shape=(
            jax.ShapeDtypeStruct(adjoint.shape, F32),
            jax.ShapeDtypeStruct((axial // 2, 2, sector, 2 * vertices), BF16),
        ),
        in_specs=[
            pl.BlockSpec(memory_space=pl.ANY),
            pl.BlockSpec((comps, planes, sector, radial), lambda i: (0, i, 0, 0)),
            vmem,
            vmem,
            vmem,
            vmem,
            vmem,
        ],
        out_specs=(
            pl.BlockSpec((comps, planes, sector, radial), lambda i: (0, i, 0, 0)),
            pl.BlockSpec(
                (planes, 1, sector, 2 * vertices),
                lambda i: (i % (steps // 2), i // (steps // 2), 0, 0),
            ),
        ),
        scratch_shapes=[
            pltpu.VMEM((comps, axial + 2, sector + 2 * PAD, radial), F32),
            pltpu.VMEM((axial + 1, sector, vertices), F32),
            pltpu.SemaphoreType.DMA((axial,)),
        ],
        compiler_params=pltpu.CompilerParams(vmem_limit_bytes=60 * 2**20),
        cost_estimate=pl.CostEstimate(
            flops=60 * adjoint.size, bytes_accessed=14 * adjoint.size, transcendentals=0
        ),
        name="stencil",
    )(adjoint, primal, wall, *halos)


def smooth_kernel(
    n_ax,
    n_az,
    tiles_in,
    owner,
    adjacency,
    counts,
    laplacian,
    out,
    tiles,
    matrices,
    pair_out,
    pair_own,
    pair_in,
    plane_sum,
    plane_in,
    axial_out,
    axial_in,
    ring_out,
    ring_in,
    tile_sem,
    matrix_sem,
    pair_sems,
    plane_sems,
    axial_sems,
    ring_sems,
):
    ax, az = lax.axis_index("ax"), lax.axis_index("az")
    patches, vertices = out.shape[1:]
    chips = n_az // 2
    chip, core = az // 2, az % 2
    sibling = chip * 2 + (1 - core)
    after, before = (az + 1) % n_az, (az + n_az - 1) % n_az
    half_rows = chips * patches

    tile_load = pltpu.make_async_copy(tiles_in, tiles, tile_sem)
    tile_load.start()
    load = pltpu.make_async_copy(laplacian, matrices, matrix_sem)
    load.start()

    barrier = pltpu.get_barrier_semaphore()
    partners = [(ax, sibling), (ax, after), (ax, before)]
    partners += [(ax, ((chip + d) % chips) * 2 + core) for d in range(1, chips)]
    partners += [((ax + d) % n_ax, az) for d in range(1, n_ax)]
    for partner in partners:
        pl.semaphore_signal(barrier, inc=1, device_id=partner, device_id_type=MESH)

    columns_half = owner.shape[0] // 2
    owners = jnp.concatenate([owner[:columns_half, :], owner[columns_half:, :]], axis=1)
    width = owners.shape[1]
    row = lax.broadcasted_iota(jnp.int32, (2 * half_rows, width), 0)
    row_core = jnp.where(row < half_rows, 1 - core, core)
    row_chip = (row % half_rows) // patches
    row_patch = (row_chip * 2 + row_core) * patches + row % patches

    def partial_sum(target_ax, first):
        ids = row_patch + target_ax * n_az * patches
        hits = [
            jnp.where(ids == owners[b : b + 1, :], 1.0, 0.0).astype(BF16)
            for b in range(columns_half)
        ]
        if first:
            tile_load.wait()
        both = jnp.dot(jnp.concatenate(hits, axis=1), tiles[...], preferred_element_type=F32)
        return both[:, :vertices] + both[:, vertices:]

    def remote(src, dst, sems, target):
        return pltpu.make_async_remote_copy(
            src_ref=src,
            dst_ref=dst,
            send_sem=sems.at[0],
            recv_sem=sems.at[1],
            device_id=target,
            device_id_type=MESH,
        )

    def pair_copy(t):
        return remote(pair_out.at[t], pair_in.at[t], pair_sems.at[t], (ax, sibling))

    def plane_copy(t, d):
        target = (chip + d) % chips
        return remote(
            plane_sum.at[t, target],
            plane_in.at[t, d - 1],
            plane_sems.at[t, d - 1],
            (ax, target * 2 + core),
        )

    def axial_copy(t):
        return remote(
            axial_out.at[t], axial_in.at[t], axial_sems.at[t], ((ax + 1 + t) % n_ax, az)
        )

    def plane_stage(t):
        pair_copy(t).wait()
        joined = pair_own[t] + pair_in[t]
        plane_sum[t] = joined.reshape(chips, patches, vertices)
        for d in range(1, chips):
            plane_copy(t, d).start()

    def axial_stage(t):
        for d in range(1, chips):
            plane_copy(t, d).wait()
        total = plane_sum[t, chip]
        for d in range(1, chips):
            total += plane_in[t, d - 1]
        axial_out[t] = total
        if t < n_ax - 1:
            axial_copy(t).start()

    for t in range(n_ax):
        target_ax = (ax + 1 + t) % n_ax
        partial = partial_sum(target_ax, t == 0)
        pair_out[t] = partial[:half_rows]
        pair_own[t] = partial[half_rows:]
        if t == 0:
            pl.semaphore_wait(barrier, len(partners))
        pair_copy(t).start()
        if t >= 1:
            plane_stage(t - 1)
        if t >= 2:
            axial_stage(t - 2)
    plane_stage(n_ax - 1)
    axial_stage(n_ax - 2)

    load.wait()
    vertex = lax.broadcasted_iota(jnp.int32, (patches, vertices), 1).astype(F32)
    live = vertex < column_of(counts[...].astype(F32))
    entries = adjacency[0]
    neighbours_each = entries.shape[1]
    index = lax.broadcasted_iota(jnp.int32, (patches, 3 * patches), 1)
    incidence = jnp.zeros((patches, 3 * patches), F32)
    for e in range(neighbours_each):
        incidence += jnp.where(index == entries[:, e : e + 1], 1.0, 0.0)
    incidence = incidence.astype(BF16)
    sub = lax.broadcasted_iota(jnp.int32, (8, vertices), 0)

    axial_stage(n_ax - 1)
    total = axial_out[n_ax - 1]
    for t in range(n_ax - 1):
        axial_copy(t).wait()
        total += axial_in[t]
    source = total * wall_scale

    def ring_copies(sweep):
        return (
            remote(ring_out.at[sweep], ring_in.at[sweep, 0], ring_sems.at[sweep, 0], (ax, after)),
            remote(ring_out.at[sweep], ring_in.at[sweep, 1], ring_sems.at[sweep, 1], (ax, before)),
        )

    field = jnp.where(live, source, 0.0)
    for sweep in range(SWEEPS):
        ring_out[sweep] = field
        for copy in ring_copies(sweep):
            copy.start()
        high, low = pieces(field)
        groups = []
        for g in range(0, patches, 8):
            stack = jnp.concatenate([high[g : g + 8], low[g : g + 8]], axis=0)
            stack = jnp.concatenate([stack, stack], axis=1).astype(BF16)
            products = jnp.dot(
                stack,
                matrices[:, g * vertices : (g + 8) * vertices],
                preferred_element_type=F32,
            )
            products = products[:8] + products[8:]
            chosen = jnp.zeros((8, vertices), F32)
            for p in range(8):
                chosen = jnp.where(sub == p, products[:, p * vertices : (p + 1) * vertices], chosen)
            groups.append(chosen)
        applied = jnp.concatenate(groups, axis=0)
        for copy in ring_copies(sweep):
            copy.wait()
        around = jnp.concatenate([ring_in[sweep, 0], field, ring_in[sweep, 1]], axis=0)
        around = jnp.concatenate(pieces(around), axis=1).astype(BF16)
        near = jnp.dot(incidence, around, preferred_element_type=F32)
        near = near[:, :vertices] + near[:, vertices:]
        image = field + smoothing * (applied + coupling * (neighbours_each * field - near))
        field = jnp.where(live, field + relaxation * (source - image), 0.0)
    out[0] = field


def smooth(tiles, owner, adjacency, counts, laplacian, vertices):
    n_ax, n_az = lax.axis_size("ax"), lax.axis_size("az")
    patches = laplacian.shape[1] // vertices
    chips = n_az // 2
    block = (patches, vertices)
    half = (chips * patches, vertices)
    vmem = pl.BlockSpec(memory_space=pltpu.VMEM)
    anywhere = pl.BlockSpec(memory_space=pl.ANY)
    dma = pltpu.SemaphoreType.DMA
    return pl.pallas_call(
        functools.partial(smooth_kernel, n_ax, n_az),
        out_shape=jax.ShapeDtypeStruct((1,) + block, F32),
        in_specs=[anywhere, vmem, vmem, vmem, anywhere],
        out_specs=vmem,
        scratch_shapes=[
            pltpu.VMEM(tiles.shape, BF16),
            pltpu.VMEM(laplacian.shape, BF16),
            pltpu.VMEM((n_ax,) + half, F32),
            pltpu.VMEM((n_ax,) + half, F32),
            pltpu.VMEM((n_ax,) + half, F32),
            pltpu.VMEM((n_ax, chips) + block, F32),
            pltpu.VMEM((n_ax, chips - 1) + block, F32),
            pltpu.VMEM((n_ax,) + block, F32),
            pltpu.VMEM((n_ax,) + block, F32),
            pltpu.VMEM((SWEEPS,) + block, F32),
            pltpu.VMEM((SWEEPS, 2) + block, F32),
            dma,
            dma,
            dma((n_ax, 2)),
            dma((n_ax, chips - 1, 2)),
            dma((n_ax, 2)),
            dma((SWEEPS, 2, 2)),
        ],
        compiler_params=pltpu.CompilerParams(
            collective_id=0, has_side_effects=True, vmem_limit_bytes=60 * 2**20
        ),
        name="smooth",
    )(tiles, owner, adjacency, counts, laplacian)


def halo_kernel(
    n_ax,
    n_az,
    adjoint,
    wall,
    laplacian,
    x_low,
    x_high,
    a_low,
    a_high,
    pieces_out,
    x_in,
    a_in,
    a_out,
    x_wall,
    a_wall,
    matrices,
    matrix_sem,
    stage_sems,
    x_sems,
    a_sems,
):
    ax, az = lax.axis_index("ax"), lax.axis_index("az")
    axial, sector, radial = adjoint.shape[1:]
    patches, vertices = laplacian.shape[1:3]
    above, below = ((ax + 1) % n_ax, az), ((ax + n_ax - 1) % n_ax, az)
    after, before = (ax, (az + 1) % n_az), (ax, (az + n_az - 1) % n_az)

    load = pltpu.make_async_copy(laplacian.at[0], matrices, matrix_sem)
    gathers = [
        pltpu.make_async_copy(adjoint.at[:, :, at], a_out.at[side], stage_sems.at[side])
        for side, at in enumerate((sector - 1, 0))
    ]
    for gather in gathers:
        gather.start()
    barrier = pltpu.get_barrier_semaphore()
    for partner in (above, below, after, before):
        pl.semaphore_signal(barrier, inc=1, device_id=partner, device_id_type=MESH)
    pl.semaphore_wait(barrier, 4)

    def remote(src, dst, sems, target):
        return pltpu.make_async_remote_copy(
            src_ref=src,
            dst_ref=dst,
            send_sem=sems.at[0],
            recv_sem=sems.at[1],
            device_id=target,
            device_id_type=MESH,
        )

    def x_copies(side):
        layer = adjoint.at[:, axial - 1] if side == 0 else adjoint.at[:, 0]
        target = above if side == 0 else below
        return (
            remote(layer, x_in.at[side], x_sems.at[side, 0], target),
            remote(wall, x_wall.at[side], x_sems.at[side, 1], target),
        )

    def a_copies(side):
        target = after if side == 0 else before
        return (
            remote(a_out.at[side], a_in.at[side], a_sems.at[side, 0], target),
            remote(wall, a_wall.at[side], a_sems.at[side, 1], target),
        )

    sends = (ax < n_ax - 1, ax > 0)
    takes = (ax > 0, ax < n_ax - 1)
    for side in range(2):

        @pl.when(sends[side])
        def _():
            for copy in x_copies(side):
                copy.start()

    for side in range(2):
        gathers[side].wait()
        for copy in a_copies(side):
            copy.start()

    load.start()
    load.wait()

    def split(p, carry):
        high, low = pieces(matrices[p].T)
        at = pl.multiple_of(p * vertices, vertices)
        pieces_out[:vertices, pl.ds(at, vertices)] = high.astype(BF16)
        pieces_out[vertices:, pl.ds(at, vertices)] = low.astype(BF16)
        return carry

    lax.fori_loop(0, patches, split, 0, unroll=4)

    lane = lax.broadcasted_iota(jnp.int32, (axial, radial), 1)
    for side, (target, at) in enumerate(((a_low, sector - 1), (a_high, 0))):
        for copy in a_copies(side):
            copy.wait()
        fluid = lane >= a_wall[side][:, at : at + 1]
        for c in range(3):
            target[c] = jnp.where(fluid, a_in[side, c], 0.0)

    lane = lax.broadcasted_iota(jnp.int32, (sector, radial), 1).astype(F32)
    for side, (target, at) in enumerate(((x_low, axial - 1), (x_high, 0))):

        @pl.when(sends[side])
        def _():
            for copy in x_copies(side):
                copy.wait_send()

        @pl.when(takes[side])
        def _():
            for copy in x_copies(side):
                copy.wait_recv()
            fluid = lane >= column_of(x_wall[side][at : at + 1, :].astype(F32))
            for c in range(3):
                target[c] = jnp.where(fluid, x_in[side, c], 0.0)

        @pl.when(jnp.logical_not(takes[side]))
        def _():
            target[...] = jnp.zeros(target.shape, F32)


def halos(adjoint, wall, laplacian):
    n_ax, n_az = lax.axis_size("ax"), lax.axis_size("az")
    comps, axial, sector, radial = adjoint.shape
    patches, vertices = laplacian.shape[1:3]
    vmem = pl.BlockSpec(memory_space=pltpu.VMEM)
    anywhere = pl.BlockSpec(memory_space=pl.ANY)
    dma = pltpu.SemaphoreType.DMA
    x_layer = (comps, sector, radial)
    a_layer = (comps, axial, radial)
    return pl.pallas_call(
        functools.partial(halo_kernel, n_ax, n_az),
        out_shape=(
            jax.ShapeDtypeStruct(x_layer, F32),
            jax.ShapeDtypeStruct(x_layer, F32),
            jax.ShapeDtypeStruct(a_layer, F32),
            jax.ShapeDtypeStruct(a_layer, F32),
            jax.ShapeDtypeStruct((2 * vertices, patches * vertices), BF16),
        ),
        in_specs=[anywhere, vmem, anywhere],
        out_specs=(vmem,) * 5,
        scratch_shapes=[
            pltpu.VMEM((2,) + x_layer, F32),
            pltpu.VMEM((2,) + a_layer, F32),
            pltpu.VMEM((2,) + a_layer, F32),
            pltpu.VMEM((2,) + wall.shape, jnp.int32),
            pltpu.VMEM((2,) + wall.shape, jnp.int32),
            pltpu.VMEM(laplacian.shape[1:], F32),
            dma,
            dma((2,)),
            dma((2, 2, 2)),
            dma((2, 2, 2)),
        ],
        compiler_params=pltpu.CompilerParams(
            collective_id=1, has_side_effects=True, vmem_limit_bytes=60 * 2**20
        ),
        name="halos",
    )(adjoint, wall, laplacian)


def shards(adjoint, primal, wall, owner, adjacency, counts, laplacian):
    vertices = laplacian.shape[2]
    *layers, matrices = halos(adjoint, wall, laplacian)
    updated, tiles = stencil(adjoint, primal, wall, layers, vertices)
    tiles = tiles.reshape(-1, 2 * vertices)
    return updated, smooth(tiles, owner, adjacency, counts, matrices, vertices)


def solution(mesh):
    in_specs = (
        P(None, "ax", "az", None),
        P(None, "ax", "az", None),
        P("ax", "az"),
        P("ax", "az"),
        P("ax", "az", None),
        P("ax", "az"),
        P("ax", "az", None, None),
    )
    out_specs = (P(None, "ax", "az", None), P("ax", "az", None))
    return jax.shard_map(shards, mesh=mesh, in_specs=in_specs, out_specs=out_specs, check_vma=False)
```

```python
import functools

import jax
import jax.numpy as jnp
from jax import lax
from jax.experimental import pallas as pl
from jax.experimental.pallas import tpu as pltpu
from jax.sharding import PartitionSpec as P

SWEEPS = 3

time_step = 0.12
viscosity = 1.0
wall_scale = 0.1
smoothing = 0.5
coupling = 0.25
relaxation = 0.25

F32 = jnp.float32
BF16 = jnp.bfloat16
MESH = pl.DeviceIdType.MESH
PAD = 8


def pieces(value):
    high = value.astype(BF16).astype(F32)
    return high, value - high


def column_of(row):
    n = row.shape[1]
    eye = lax.broadcasted_iota(jnp.int32, (n, n), 0) == lax.broadcasted_iota(jnp.int32, (n, n), 1)
    return jnp.sum(jnp.where(eye, jnp.broadcast_to(row, (n, n)), 0.0), axis=1, keepdims=True)


def stencil_kernel(
    planes,
    adjoint,
    primal,
    wall,
    owner,
    x_low,
    x_high,
    a_low,
    a_high,
    out,
    sums,
    held,
    depth_of,
    tiles,
    sems,
):
    step = pl.program_id(0)
    axial, sector, radial = adjoint.shape[1:]
    vertices = sums.shape[1]
    rows = 8

    def fetch(x):
        return pltpu.make_async_copy(
            adjoint.at[:, x], held.at[:, x + 1, pl.ds(PAD, sector), :], sems.at[x]
        )

    def side_rows(x):
        for c in range(3):
            held[c, x + 1, PAD - 1 : PAD, :] = a_low[c, pl.ds(x, 1), :]
            held[c, x + 1, PAD + sector : PAD + sector + 1, :] = a_high[c, pl.ds(x, 1), :]

    @pl.when(step == 0)
    def _():
        def begin(x, carry):
            fetch(x).start()
            return carry

        lax.fori_loop(0, axial, begin, 0)
        for c in range(3):
            held[c, 0, PAD : PAD + sector, :] = x_low[c]
            held[c, axial + 1, PAD : PAD + sector, :] = x_high[c]
        depths = wall[...].astype(F32)
        for x in range(axial):
            column = column_of(depths[x : x + 1, :])
            depth_of[x] = jnp.broadcast_to(column, depth_of.shape[1:])
        depth_of[axial] = jnp.zeros(depth_of.shape[1:], F32)
        fetch(0).wait()
        side_rows(0)
        full_lane = lax.broadcasted_iota(jnp.int32, (sector, radial), 1).astype(F32)
        solid = full_lane < jnp.concatenate([depth_of[0]] * (radial // vertices), axis=1)
        for c in range(3):
            body = held[c, 1, PAD : PAD + sector, :]
            held[c, 1, PAD : PAD + sector, :] = jnp.where(solid, 0.0, body)

    lane = lax.broadcasted_iota(jnp.int32, (rows, radial), 1)
    sub = lax.broadcasted_iota(jnp.int32, (rows, radial), 0)
    first, last = lane == 0, lane == radial - 1
    top, bottom = sub == 0, sub == rows - 1
    lane_value = lane.astype(F32)

    def plane(j, carry):
        x = step * planes + j

        @pl.when(x + 1 < axial)
        def _():
            fetch(x + 1).wait()
            side_rows(x + 1)

        def fluid_at(x, a):
            depth = depth_of[x, a : a + rows, :]
            return lane_value >= jnp.concatenate([depth] * (radial // vertices), axis=1)

        def block(c, at):
            return held[c, x + 1, at : at + rows, :]

        middles = [block(c, PAD) for c in range(3)]
        downs = [pltpu.roll(block(c, PAD - rows), 1, 0) for c in range(3)]
        ups = [pltpu.roll(middles[c], rows - 1, 0) for c in range(3)]
        highs, lows = [], []
        for a in range(0, sector, rows):
            at = PAD + a
            fluid, fluid_next = fluid_at(x, a), fluid_at(x + 1, a)
            flows = [primal[d, j, a : a + rows, :] for d in range(3)]
            half = [(0.5 * time_step) * flow for flow in flows]
            plus = [viscosity * time_step + value for value in half]
            minus = [viscosity * time_step - value for value in half]
            plus[2] = jnp.where(last, 0.0, plus[2])
            minus[2] = jnp.where(first, 0.0, minus[2])
            total = jnp.zeros((rows, vertices), F32)
            for c in range(3):
                middle = middles[c]
                follow = block(c, at + rows)
                down = pltpu.roll(middle, 1, 0)
                up = pltpu.roll(follow, rows - 1, 0)
                value = (1.0 - 6.0 * viscosity * time_step) * middle
                ahead = jnp.where(fluid_next, held[c, x + 2, at : at + rows, :], 0.0)
                held[c, x + 2, at : at + rows, :] = ahead
                value += plus[0] * ahead
                value += minus[0] * held[c, x, at : at + rows, :]
                value += plus[1] * jnp.where(bottom, up, ups[c])
                value += minus[1] * jnp.where(top, downs[c], down)
                value += plus[2] * pltpu.roll(middle, radial - 1, 1)
                value += minus[2] * pltpu.roll(middle, 1, 1)
                value = jnp.where(fluid, value, 0.0)
                out[c, j, a : a + rows, :] = value
                total += flows[c][:, :vertices] * value[:, :vertices]
                middles[c], downs[c], ups[c] = follow, down, up
            high, low = pieces(total)
            highs.append(high)
            lows.append(low)
        both = [jnp.concatenate(part, axis=0) for part in (highs, lows)]
        at = pl.multiple_of(j * sector, sector)
        tiles[pl.ds(at, sector), :] = jnp.concatenate(both, axis=1).astype(BF16)
        return carry

    lax.fori_loop(0, planes, plane, 0)

    owners = [owner[pl.ds(step * planes + j, 1), :] for j in range(planes)]
    owners = jnp.concatenate(owners, axis=1)
    chunk = 256
    row = lax.broadcasted_iota(jnp.int32, (chunk, planes * sector), 0)
    for at in range(0, sums.shape[0], chunk):
        hits = jnp.where(row + at == owners, 1.0, 0.0).astype(BF16)
        both = jnp.dot(hits, tiles[...], preferred_element_type=F32)
        both = both[:, :vertices] + both[:, vertices:]
        sums[at : at + chunk, :] = both + jnp.where(step > 0, sums[at : at + chunk, :], 0.0)


def stencil(adjoint, primal, wall, owner, halos, patches_all, vertices):
    comps, axial, sector, radial = adjoint.shape
    planes = 4
    steps = axial // planes
    vmem = pl.BlockSpec(memory_space=pltpu.VMEM)
    return pl.pallas_call(
        functools.partial(stencil_kernel, planes),
        grid=(steps,),
        out_shape=(
            jax.ShapeDtypeStruct(adjoint.shape, F32),
            jax.ShapeDtypeStruct((patches_all, vertices), F32),
        ),
        in_specs=[
            pl.BlockSpec(memory_space=pl.ANY),
            pl.BlockSpec((comps, planes, sector, radial), lambda i: (0, i, 0, 0)),
            vmem,
            vmem,
            vmem,
            vmem,
            vmem,
            vmem,
        ],
        out_specs=(
            pl.BlockSpec((comps, planes, sector, radial), lambda i: (0, i, 0, 0)),
            pl.BlockSpec((patches_all, vertices), lambda i: (0, 0)),
        ),
        scratch_shapes=[
            pltpu.VMEM((comps, axial + 2, sector + 2 * PAD, radial), F32),
            pltpu.VMEM((axial + 1, sector, vertices), F32),
            pltpu.VMEM((planes * sector, 2 * vertices), BF16),
            pltpu.SemaphoreType.DMA((axial,)),
        ],
        compiler_params=pltpu.CompilerParams(vmem_limit_bytes=46 * 2**20),
        cost_estimate=pl.CostEstimate(
            flops=60 * adjoint.size, bytes_accessed=14 * adjoint.size, transcendentals=0
        ),
        name="stencil",
    )(adjoint, primal, wall, owner, *halos)


def smooth_kernel(
    n_ax,
    n_az,
    sums,
    adjacency,
    counts,
    laplacian,
    out,
    matrices,
    pair_in,
    plane_sum,
    plane_in,
    axial_out,
    axial_in,
    ring_out,
    ring_in,
    matrix_sem,
    pair_sems,
    plane_sems,
    axial_sems,
    ring_sems,
):
    ax, az = lax.axis_index("ax"), lax.axis_index("az")
    patches, vertices = out.shape[1:]
    chips = n_az // 2
    chip, core = az // 2, az % 2
    sibling = chip * 2 + (1 - core)
    after, before = (az + 1) % n_az, (az + n_az - 1) % n_az

    load = pltpu.make_async_copy(laplacian, matrices, matrix_sem)
    load.start()

    barrier = pltpu.get_barrier_semaphore()
    partners = [(ax, sibling), (ax, after), (ax, before)]
    partners += [(ax, ((chip + d) % chips) * 2 + core) for d in range(1, chips)]
    partners += [((ax + d) % n_ax, az) for d in range(1, n_ax)]
    for partner in partners:
        pl.semaphore_signal(barrier, inc=1, device_id=partner, device_id_type=MESH)

    def remote(src, dst, sems, target):
        return pltpu.make_async_remote_copy(
            src_ref=src,
            dst_ref=dst,
            send_sem=sems.at[0],
            recv_sem=sems.at[1],
            device_id=target,
            device_id_type=MESH,
        )

    def pair_copy(t):
        layer = sums.at[(ax + 1 + t) % n_ax, :, 1 - core]
        return remote(layer, pair_in.at[t], pair_sems.at[t], (ax, sibling))

    def plane_copy(t, d):
        target = (chip + d) % chips
        return remote(
            plane_sum.at[t, target],
            plane_in.at[t, d - 1],
            plane_sems.at[t, d - 1],
            (ax, target * 2 + core),
        )

    def axial_copy(t):
        return remote(
            axial_out.at[t], axial_in.at[t], axial_sems.at[t], ((ax + 1 + t) % n_ax, az)
        )

    def plane_stage(t):
        pair_copy(t).wait()
        plane_sum[t] = sums[(ax + 1 + t) % n_ax, :, core] + pair_in[t]
        for d in range(1, chips):
            plane_copy(t, d).start()

    def axial_stage(t):
        for d in range(1, chips):
            plane_copy(t, d).wait()
        total = plane_sum[t, chip]
        for d in range(1, chips):
            total += plane_in[t, d - 1]
        axial_out[t] = total
        if t < n_ax - 1:
            axial_copy(t).start()

    pl.semaphore_wait(barrier, len(partners))
    for t in range(n_ax):
        pair_copy(t).start()
    for t in range(n_ax):
        plane_stage(t)
        if t >= 1:
            axial_stage(t - 1)

    load.wait()
    vertex = lax.broadcasted_iota(jnp.int32, (patches, vertices), 1).astype(F32)
    live = vertex < column_of(counts[...].astype(F32))
    entries = adjacency[0]
    neighbours_each = entries.shape[1]
    index = lax.broadcasted_iota(jnp.int32, (patches, 3 * patches), 1)
    incidence = jnp.zeros((patches, 3 * patches), F32)
    for e in range(neighbours_each):
        incidence += jnp.where(index == entries[:, e : e + 1], 1.0, 0.0)
    incidence = incidence.astype(BF16)
    sub = lax.broadcasted_iota(jnp.int32, (8, vertices), 0)

    axial_stage(n_ax - 1)
    total = axial_out[n_ax - 1]
    for t in range(n_ax - 1):
        axial_copy(t).wait()
        total += axial_in[t]
    source = total * wall_scale

    def ring_copies(sweep):
        return (
            remote(ring_out.at[sweep], ring_in.at[sweep, 0], ring_sems.at[sweep, 0], (ax, after)),
            remote(ring_out.at[sweep], ring_in.at[sweep, 1], ring_sems.at[sweep, 1], (ax, before)),
        )

    field = jnp.where(live, source, 0.0)
    for sweep in range(SWEEPS):
        ring_out[sweep] = field
        for copy in ring_copies(sweep):
            copy.start()
        high, low = pieces(field)
        groups = []
        for g in range(0, patches, 8):
            stack = jnp.concatenate([high[g : g + 8], low[g : g + 8]], axis=0)
            stack = jnp.concatenate([stack, stack], axis=1).astype(BF16)
            products = jnp.dot(
                stack,
                matrices[:, g * vertices : (g + 8) * vertices],
                preferred_element_type=F32,
            )
            products = products[:8] + products[8:]
            chosen = jnp.zeros((8, vertices), F32)
            for p in range(8):
                chosen = jnp.where(sub == p, products[:, p * vertices : (p + 1) * vertices], chosen)
            groups.append(chosen)
        applied = jnp.concatenate(groups, axis=0)
        for copy in ring_copies(sweep):
            copy.wait()
        around = jnp.concatenate([ring_in[sweep, 0], field, ring_in[sweep, 1]], axis=0)
        around = jnp.concatenate(pieces(around), axis=1).astype(BF16)
        near = jnp.dot(incidence, around, preferred_element_type=F32)
        near = near[:, :vertices] + near[:, vertices:]
        image = field + smoothing * (applied + coupling * (neighbours_each * field - near))
        field = jnp.where(live, field + relaxation * (source - image), 0.0)
    out[0] = field


def smooth(sums, adjacency, counts, laplacian):
    n_ax, n_az = lax.axis_size("ax"), lax.axis_size("az")
    chips = n_az // 2
    patches, vertices = counts.shape[1], sums.shape[1]
    sums = sums.reshape(n_ax, chips, 2, patches, vertices)
    block = (patches, vertices)
    vmem = pl.BlockSpec(memory_space=pltpu.VMEM)
    anywhere = pl.BlockSpec(memory_space=pl.ANY)
    dma = pltpu.SemaphoreType.DMA
    return pl.pallas_call(
        functools.partial(smooth_kernel, n_ax, n_az),
        out_shape=jax.ShapeDtypeStruct((1,) + block, F32),
        in_specs=[vmem, vmem, vmem, anywhere],
        out_specs=vmem,
        scratch_shapes=[
            pltpu.VMEM(laplacian.shape, BF16),
            pltpu.VMEM((n_ax, chips) + block, F32),
            pltpu.VMEM((n_ax, chips) + block, F32),
            pltpu.VMEM((n_ax, chips - 1) + block, F32),
            pltpu.VMEM((n_ax,) + block, F32),
            pltpu.VMEM((n_ax,) + block, F32),
            pltpu.VMEM((SWEEPS,) + block, F32),
            pltpu.VMEM((SWEEPS, 2) + block, F32),
            dma,
            dma((n_ax, 2)),
            dma((n_ax, chips - 1, 2)),
            dma((n_ax, 2)),
            dma((SWEEPS, 2, 2)),
        ],
        compiler_params=pltpu.CompilerParams(
            collective_id=0, has_side_effects=True, vmem_limit_bytes=40 * 2**20
        ),
        name="smooth",
    )(sums, adjacency, counts, laplacian)


def halo_kernel(
    n_ax,
    n_az,
    adjoint,
    wall,
    laplacian,
    x_low,
    x_high,
    a_low,
    a_high,
    pieces_out,
    x_in,
    a_in,
    a_out,
    x_wall,
    a_wall,
    matrices,
    matrix_sem,
    stage_sems,
    x_sems,
    a_sems,
):
    ax, az = lax.axis_index("ax"), lax.axis_index("az")
    axial, sector, radial = adjoint.shape[1:]
    patches, vertices = laplacian.shape[1:3]
    above, below = ((ax + 1) % n_ax, az), ((ax + n_ax - 1) % n_ax, az)
    after, before = (ax, (az + 1) % n_az), (ax, (az + n_az - 1) % n_az)

    load = pltpu.make_async_copy(laplacian.at[0], matrices, matrix_sem)
    gathers = [
        pltpu.make_async_copy(adjoint.at[:, :, at], a_out.at[side], stage_sems.at[side])
        for side, at in enumerate((sector - 1, 0))
    ]
    for gather in gathers:
        gather.start()
    barrier = pltpu.get_barrier_semaphore()
    for partner in (above, below, after, before):
        pl.semaphore_signal(barrier, inc=1, device_id=partner, device_id_type=MESH)
    pl.semaphore_wait(barrier, 4)

    def remote(src, dst, sems, target):
        return pltpu.make_async_remote_copy(
            src_ref=src,
            dst_ref=dst,
            send_sem=sems.at[0],
            recv_sem=sems.at[1],
            device_id=target,
            device_id_type=MESH,
        )

    def x_copies(side):
        layer = adjoint.at[:, axial - 1] if side == 0 else adjoint.at[:, 0]
        target = above if side == 0 else below
        return (
            remote(layer, x_in.at[side], x_sems.at[side, 0], target),
            remote(wall, x_wall.at[side], x_sems.at[side, 1], target),
        )

    def a_copies(side):
        target = after if side == 0 else before
        return (
            remote(a_out.at[side], a_in.at[side], a_sems.at[side, 0], target),
            remote(wall, a_wall.at[side], a_sems.at[side, 1], target),
        )

    sends = (ax < n_ax - 1, ax > 0)
    takes = (ax > 0, ax < n_ax - 1)
    for side in range(2):

        @pl.when(sends[side])
        def _():
            for copy in x_copies(side):
                copy.start()

    for side in range(2):
        gathers[side].wait()
        for copy in a_copies(side):
            copy.start()

    load.start()
    load.wait()

    def split(p, carry):
        high, low = pieces(matrices[p].T)
        at = pl.multiple_of(p * vertices, vertices)
        pieces_out[:vertices, pl.ds(at, vertices)] = high.astype(BF16)
        pieces_out[vertices:, pl.ds(at, vertices)] = low.astype(BF16)
        return carry

    lax.fori_loop(0, patches, split, 0, unroll=4)

    lane = lax.broadcasted_iota(jnp.int32, (axial, radial), 1)
    for side, (target, at) in enumerate(((a_low, sector - 1), (a_high, 0))):
        for copy in a_copies(side):
            copy.wait()
        fluid = lane >= a_wall[side][:, at : at + 1]
        for c in range(3):
            target[c] = jnp.where(fluid, a_in[side, c], 0.0)

    lane = lax.broadcasted_iota(jnp.int32, (sector, radial), 1).astype(F32)
    for side, (target, at) in enumerate(((x_low, axial - 1), (x_high, 0))):

        @pl.when(sends[side])
        def _():
            for copy in x_copies(side):
                copy.wait_send()

        @pl.when(takes[side])
        def _():
            for copy in x_copies(side):
                copy.wait_recv()
            fluid = lane >= column_of(x_wall[side][at : at + 1, :].astype(F32))
            for c in range(3):
                target[c] = jnp.where(fluid, x_in[side, c], 0.0)

        @pl.when(jnp.logical_not(takes[side]))
        def _():
            target[...] = jnp.zeros(target.shape, F32)


def halos(adjoint, wall, laplacian):
    n_ax, n_az = lax.axis_size("ax"), lax.axis_size("az")
    comps, axial, sector, radial = adjoint.shape
    patches, vertices = laplacian.shape[1:3]
    vmem = pl.BlockSpec(memory_space=pltpu.VMEM)
    anywhere = pl.BlockSpec(memory_space=pl.ANY)
    dma = pltpu.SemaphoreType.DMA
    x_layer = (comps, sector, radial)
    a_layer = (comps, axial, radial)
    return pl.pallas_call(
        functools.partial(halo_kernel, n_ax, n_az),
        out_shape=(
            jax.ShapeDtypeStruct(x_layer, F32),
            jax.ShapeDtypeStruct(x_layer, F32),
            jax.ShapeDtypeStruct(a_layer, F32),
            jax.ShapeDtypeStruct(a_layer, F32),
            jax.ShapeDtypeStruct((2 * vertices, patches * vertices), BF16),
        ),
        in_specs=[anywhere, vmem, anywhere],
        out_specs=(vmem,) * 5,
        scratch_shapes=[
            pltpu.VMEM((2,) + x_layer, F32),
            pltpu.VMEM((2,) + a_layer, F32),
            pltpu.VMEM((2,) + a_layer, F32),
            pltpu.VMEM((2,) + wall.shape, jnp.int32),
            pltpu.VMEM((2,) + wall.shape, jnp.int32),
            pltpu.VMEM(laplacian.shape[1:], F32),
            dma,
            dma((2,)),
            dma((2, 2, 2)),
            dma((2, 2, 2)),
        ],
        compiler_params=pltpu.CompilerParams(
            collective_id=1, has_side_effects=True, vmem_limit_bytes=57 * 2**20
        ),
        cost_estimate=pl.CostEstimate(
            flops=0, bytes_accessed=8 * adjoint.size * 4, transcendentals=0
        ),
        name="halos",
    )(adjoint, wall, laplacian)


def shards(adjoint, primal, wall, owner, adjacency, counts, laplacian):
    vertices = laplacian.shape[2]
    *layers, matrices = halos(adjoint, wall, laplacian)
    patches_all = lax.axis_size("ax") * lax.axis_size("az") * laplacian.shape[1]
    updated, sums = stencil(adjoint, primal, wall, owner, layers, patches_all, vertices)
    return updated, smooth(sums, adjacency, counts, matrices)


def solution(mesh):
    in_specs = (
        P(None, "ax", "az", None),
        P(None, "ax", "az", None),
        P("ax", "az"),
        P("ax", "az"),
        P("ax", "az", None),
        P("ax", "az"),
        P("ax", "az", None, None),
    )
    out_specs = (P(None, "ax", "az", None), P("ax", "az", None))
    return jax.shard_map(shards, mesh=mesh, in_specs=in_specs, out_specs=out_specs, check_vma=False)
```

```python
import functools

import jax
import jax.numpy as jnp
from jax import lax
from jax.experimental import pallas as pl
from jax.experimental.pallas import tpu as pltpu
from jax.sharding import PartitionSpec as P

SWEEPS = 3

time_step = 0.12
viscosity = 1.0
wall_scale = 0.1
smoothing = 0.5
coupling = 0.25
relaxation = 0.25

F32 = jnp.float32
BF16 = jnp.bfloat16
MESH = pl.DeviceIdType.MESH
PAD = 8


def pieces(value):
    high = value.astype(BF16).astype(F32)
    return high, value - high


def column_of(row):
    n = row.shape[1]
    eye = lax.broadcasted_iota(jnp.int32, (n, n), 0) == lax.broadcasted_iota(jnp.int32, (n, n), 1)
    return jnp.sum(jnp.where(eye, jnp.broadcast_to(row, (n, n)), 0.0), axis=1, keepdims=True)


def stencil_kernel(
    planes, adjoint, primal, wall, x_low, x_high, a_low, a_high, out, tiles, held, depth_of, sems
):
    step = pl.program_id(0)
    axial, sector, radial = adjoint.shape[1:]
    vertices = tiles.shape[-1] // 2
    rows = 8

    def fetch(x):
        return pltpu.make_async_copy(
            adjoint.at[:, x], held.at[:, x + 1, pl.ds(PAD, sector), :], sems.at[x]
        )

    def side_rows(x):
        for c in range(3):
            held[c, x + 1, PAD - 1 : PAD, :] = a_low[c, pl.ds(x, 1), :]
            held[c, x + 1, PAD + sector : PAD + sector + 1, :] = a_high[c, pl.ds(x, 1), :]

    def begin(x, carry):
        fetch(x).start()
        return carry

    @pl.when(step == 0)
    def _():
        lax.fori_loop(0, min(axial, 2 * planes + 1), begin, 0)
        for c in range(3):
            held[c, 0, PAD : PAD + sector, :] = x_low[c]
            held[c, axial + 1, PAD : PAD + sector, :] = x_high[c]
        depths = wall[...].astype(F32)
        for x in range(axial):
            column = column_of(depths[x : x + 1, :])
            depth_of[x] = jnp.broadcast_to(column, depth_of.shape[1:])
        depth_of[axial] = jnp.zeros(depth_of.shape[1:], F32)
        fetch(0).wait()
        side_rows(0)
        full_lane = lax.broadcasted_iota(jnp.int32, (sector, radial), 1).astype(F32)
        solid = full_lane < jnp.concatenate([depth_of[0]] * (radial // vertices), axis=1)
        for c in range(3):
            body = held[c, 1, PAD : PAD + sector, :]
            held[c, 1, PAD : PAD + sector, :] = jnp.where(solid, 0.0, body)

    for j in range(1, planes + 1):
        later = (step + 2) * planes + j

        @pl.when(later < axial)
        def _():
            fetch(later).start()

    lane = lax.broadcasted_iota(jnp.int32, (rows, radial), 1)
    sub = lax.broadcasted_iota(jnp.int32, (rows, radial), 0)
    first, last = lane == 0, lane == radial - 1
    top, bottom = sub == 0, sub == rows - 1
    lane_value = lane.astype(F32)

    def plane(j, carry):
        x = step * planes + j

        @pl.when(x + 1 < axial)
        def _():
            fetch(x + 1).wait()
            side_rows(x + 1)

        def fluid_at(x, a):
            depth = depth_of[x, a : a + rows, :]
            return lane_value >= jnp.concatenate([depth] * (radial // vertices), axis=1)

        def block(c, at):
            return held[c, x + 1, at : at + rows, :]

        middles = [block(c, PAD) for c in range(3)]
        downs = [pltpu.roll(block(c, PAD - rows), 1, 0) for c in range(3)]
        ups = [pltpu.roll(middles[c], rows - 1, 0) for c in range(3)]
        highs, lows = [], []
        for a in range(0, sector, rows):
            at = PAD + a
            fluid, fluid_next = fluid_at(x, a), fluid_at(x + 1, a)
            flows = [primal[d, j, a : a + rows, :] for d in range(3)]
            half = [(0.5 * time_step) * flow for flow in flows]
            plus = [viscosity * time_step + value for value in half]
            minus = [viscosity * time_step - value for value in half]
            plus[2] = jnp.where(last, 0.0, plus[2])
            minus[2] = jnp.where(first, 0.0, minus[2])
            total = jnp.zeros((rows, vertices), F32)
            for c in range(3):
                middle = middles[c]
                follow = block(c, at + rows)
                down = pltpu.roll(middle, 1, 0)
                up = pltpu.roll(follow, rows - 1, 0)
                value = (1.0 - 6.0 * viscosity * time_step) * middle
                ahead = jnp.where(fluid_next, held[c, x + 2, at : at + rows, :], 0.0)
                held[c, x + 2, at : at + rows, :] = ahead
                value += plus[0] * ahead
                value += minus[0] * held[c, x, at : at + rows, :]
                value += plus[1] * jnp.where(bottom, up, ups[c])
                value += minus[1] * jnp.where(top, downs[c], down)
                value += plus[2] * pltpu.roll(middle, radial - 1, 1)
                value += minus[2] * pltpu.roll(middle, 1, 1)
                value = jnp.where(fluid, value, 0.0)
                out[c, j, a : a + rows, :] = value
                total += flows[c][:, :vertices] * value[:, :vertices]
                middles[c], downs[c], ups[c] = follow, down, up
            high, low = pieces(total)
            highs.append(high)
            lows.append(low)
        both = [jnp.concatenate(part, axis=0) for part in (highs, lows)]
        tiles[j, 0] = jnp.concatenate(both, axis=1).astype(BF16)
        return carry

    lax.fori_loop(0, planes, plane, 0)


def stencil(adjoint, primal, wall, halos, vertices):
    comps, axial, sector, radial = adjoint.shape
    planes = 4
    steps = axial // planes
    vmem = pl.BlockSpec(memory_space=pltpu.VMEM)
    return pl.pallas_call(
        functools.partial(stencil_kernel, planes),
        grid=(steps,),
        out_shape=(
            jax.ShapeDtypeStruct(adjoint.shape, F32),
            jax.ShapeDtypeStruct((axial // 2, 2, sector, 2 * vertices), BF16),
        ),
        in_specs=[
            pl.BlockSpec(memory_space=pl.ANY),
            pl.BlockSpec((comps, planes, sector, radial), lambda i: (0, i, 0, 0)),
            vmem,
            vmem,
            vmem,
            vmem,
            vmem,
        ],
        out_specs=(
            pl.BlockSpec((comps, planes, sector, radial), lambda i: (0, i, 0, 0)),
            pl.BlockSpec(
                (planes, 1, sector, 2 * vertices),
                lambda i: (i % (steps // 2), i // (steps // 2), 0, 0),
            ),
        ),
        scratch_shapes=[
            pltpu.VMEM((comps, axial + 2, sector + 2 * PAD, radial), F32),
            pltpu.VMEM((axial + 1, sector, vertices), F32),
            pltpu.SemaphoreType.DMA((axial,)),
        ],
        compiler_params=pltpu.CompilerParams(vmem_limit_bytes=60 * 2**20),
        cost_estimate=pl.CostEstimate(
            flops=60 * adjoint.size, bytes_accessed=14 * adjoint.size, transcendentals=0
        ),
        name="stencil",
    )(adjoint, primal, wall, *halos)


def smooth_kernel(
    n_ax,
    n_az,
    tiles,
    owner,
    adjacency,
    counts,
    laplacian,
    out,
    matrices,
    pair_out,
    pair_own,
    pair_in,
    plane_sum,
    plane_in,
    axial_out,
    axial_in,
    ring_out,
    ring_in,
    matrix_sem,
    pair_sems,
    plane_sems,
    axial_sems,
    ring_sems,
):
    ax, az = lax.axis_index("ax"), lax.axis_index("az")
    patches, vertices = out.shape[1:]
    chips = n_az // 2
    chip, core = az // 2, az % 2
    sibling = chip * 2 + (1 - core)
    after, before = (az + 1) % n_az, (az + n_az - 1) % n_az
    half_rows = chips * patches

    load = pltpu.make_async_copy(laplacian, matrices, matrix_sem)
    load.start()

    barrier = pltpu.get_barrier_semaphore()
    partners = [(ax, sibling), (ax, after), (ax, before)]
    partners += [(ax, ((chip + d) % chips) * 2 + core) for d in range(1, chips)]
    partners += [((ax + d) % n_ax, az) for d in range(1, n_ax)]
    for partner in partners:
        pl.semaphore_signal(barrier, inc=1, device_id=partner, device_id_type=MESH)

    columns_half = owner.shape[0] // 2
    owners = jnp.concatenate([owner[:columns_half, :], owner[columns_half:, :]], axis=1)
    width = owners.shape[1]
    row = lax.broadcasted_iota(jnp.int32, (2 * half_rows, width), 0)
    row_core = jnp.where(row < half_rows, 1 - core, core)
    row_chip = (row % half_rows) // patches
    row_patch = (row_chip * 2 + row_core) * patches + row % patches

    def partial_sum(target_ax):
        ids = row_patch + target_ax * n_az * patches
        hits = [
            jnp.where(ids == owners[b : b + 1, :], 1.0, 0.0).astype(BF16)
            for b in range(columns_half)
        ]
        both = jnp.dot(jnp.concatenate(hits, axis=1), tiles[...], preferred_element_type=F32)
        return both[:, :vertices] + both[:, vertices:]

    def remote(src, dst, sems, target):
        return pltpu.make_async_remote_copy(
            src_ref=src,
            dst_ref=dst,
            send_sem=sems.at[0],
            recv_sem=sems.at[1],
            device_id=target,
            device_id_type=MESH,
        )

    def pair_copy(t):
        return remote(pair_out.at[t], pair_in.at[t], pair_sems.at[t], (ax, sibling))

    def plane_copy(t, d):
        target = (chip + d) % chips
        return remote(
            plane_sum.at[t, target],
            plane_in.at[t, d - 1],
            plane_sems.at[t, d - 1],
            (ax, target * 2 + core),
        )

    def axial_copy(t):
        return remote(
            axial_out.at[t], axial_in.at[t], axial_sems.at[t], ((ax + 1 + t) % n_ax, az)
        )

    def plane_stage(t):
        pair_copy(t).wait()
        joined = pair_own[t] + pair_in[t]
        plane_sum[t] = joined.reshape(chips, patches, vertices)
        for d in range(1, chips):
            plane_copy(t, d).start()

    def axial_stage(t):
        for d in range(1, chips):
            plane_copy(t, d).wait()
        total = plane_sum[t, chip]
        for d in range(1, chips):
            total += plane_in[t, d - 1]
        axial_out[t] = total
        if t < n_ax - 1:
            axial_copy(t).start()

    for t in range(n_ax):
        target_ax = (ax + 1 + t) % n_ax
        partial = partial_sum(target_ax)
        pair_out[t] = partial[:half_rows]
        pair_own[t] = partial[half_rows:]
        if t == 0:
            pl.semaphore_wait(barrier, len(partners))
        pair_copy(t).start()
        if t >= 1:
            plane_stage(t - 1)
        if t >= 2:
            axial_stage(t - 2)
    plane_stage(n_ax - 1)
    axial_stage(n_ax - 2)

    load.wait()
    vertex = lax.broadcasted_iota(jnp.int32, (patches, vertices), 1).astype(F32)
    live = vertex < column_of(counts[...].astype(F32))
    entries = adjacency[0]
    neighbours_each = entries.shape[1]
    index = lax.broadcasted_iota(jnp.int32, (patches, 3 * patches), 1)
    incidence = jnp.zeros((patches, 3 * patches), F32)
    for e in range(neighbours_each):
        incidence += jnp.where(index == entries[:, e : e + 1], 1.0, 0.0)
    incidence = incidence.astype(BF16)
    sub = lax.broadcasted_iota(jnp.int32, (8, vertices), 0)

    axial_stage(n_ax - 1)
    total = axial_out[n_ax - 1]
    for t in range(n_ax - 1):
        axial_copy(t).wait()
        total += axial_in[t]
    source = total * wall_scale

    def ring_copies(sweep):
        return (
            remote(ring_out.at[sweep], ring_in.at[sweep, 0], ring_sems.at[sweep, 0], (ax, after)),
            remote(ring_out.at[sweep], ring_in.at[sweep, 1], ring_sems.at[sweep, 1], (ax, before)),
        )

    field = jnp.where(live, source, 0.0)
    for sweep in range(SWEEPS):
        ring_out[sweep] = field
        for copy in ring_copies(sweep):
            copy.start()
        high, low = pieces(field)
        groups = []
        for g in range(0, patches, 8):
            stack = jnp.concatenate([high[g : g + 8], low[g : g + 8]], axis=0)
            stack = jnp.concatenate([stack, stack], axis=1).astype(BF16)
            products = jnp.dot(
                stack,
                matrices[:, g * vertices : (g + 8) * vertices],
                preferred_element_type=F32,
            )
            products = products[:8] + products[8:]
            chosen = jnp.zeros((8, vertices), F32)
            for p in range(8):
                chosen = jnp.where(sub == p, products[:, p * vertices : (p + 1) * vertices], chosen)
            groups.append(chosen)
        applied = jnp.concatenate(groups, axis=0)
        for copy in ring_copies(sweep):
            copy.wait()
        around = jnp.concatenate([ring_in[sweep, 0], field, ring_in[sweep, 1]], axis=0)
        around = jnp.concatenate(pieces(around), axis=1).astype(BF16)
        near = jnp.dot(incidence, around, preferred_element_type=F32)
        near = near[:, :vertices] + near[:, vertices:]
        image = field + smoothing * (applied + coupling * (neighbours_each * field - near))
        field = jnp.where(live, field + relaxation * (source - image), 0.0)
    out[0] = field


def smooth(tiles, owner, adjacency, counts, laplacian, vertices):
    n_ax, n_az = lax.axis_size("ax"), lax.axis_size("az")
    patches = laplacian.shape[1] // vertices
    chips = n_az // 2
    block = (patches, vertices)
    half = (chips * patches, vertices)
    vmem = pl.BlockSpec(memory_space=pltpu.VMEM)
    dma = pltpu.SemaphoreType.DMA
    return pl.pallas_call(
        functools.partial(smooth_kernel, n_ax, n_az),
        out_shape=jax.ShapeDtypeStruct((1,) + block, F32),
        in_specs=[vmem, vmem, vmem, vmem, pl.BlockSpec(memory_space=pl.ANY)],
        out_specs=vmem,
        scratch_shapes=[
            pltpu.VMEM(laplacian.shape, BF16),
            pltpu.VMEM((n_ax,) + half, F32),
            pltpu.VMEM((n_ax,) + half, F32),
            pltpu.VMEM((n_ax,) + half, F32),
            pltpu.VMEM((n_ax, chips) + block, F32),
            pltpu.VMEM((n_ax, chips - 1) + block, F32),
            pltpu.VMEM((n_ax,) + block, F32),
            pltpu.VMEM((n_ax,) + block, F32),
            pltpu.VMEM((SWEEPS,) + block, F32),
            pltpu.VMEM((SWEEPS, 2) + block, F32),
            dma,
            dma((n_ax, 2)),
            dma((n_ax, chips - 1, 2)),
            dma((n_ax, 2)),
            dma((SWEEPS, 2, 2)),
        ],
        compiler_params=pltpu.CompilerParams(
            collective_id=0, has_side_effects=True, vmem_limit_bytes=40 * 2**20
        ),
        name="smooth",
    )(tiles, owner, adjacency, counts, laplacian)


def halo_kernel(
    n_ax,
    n_az,
    adjoint,
    wall,
    laplacian,
    x_low,
    x_high,
    a_low,
    a_high,
    pieces_out,
    x_in,
    a_in,
    a_out,
    x_wall,
    a_wall,
    matrices,
    matrix_sem,
    stage_sems,
    x_sems,
    a_sems,
):
    ax, az = lax.axis_index("ax"), lax.axis_index("az")
    axial, sector, radial = adjoint.shape[1:]
    patches, vertices = laplacian.shape[1:3]
    above, below = ((ax + 1) % n_ax, az), ((ax + n_ax - 1) % n_ax, az)
    after, before = (ax, (az + 1) % n_az), (ax, (az + n_az - 1) % n_az)

    load = pltpu.make_async_copy(laplacian.at[0], matrices, matrix_sem)
    gathers = [
        pltpu.make_async_copy(adjoint.at[:, :, at], a_out.at[side], stage_sems.at[side])
        for side, at in enumerate((sector - 1, 0))
    ]
    for gather in gathers:
        gather.start()
    barrier = pltpu.get_barrier_semaphore()
    for partner in (above, below, after, before):
        pl.semaphore_signal(barrier, inc=1, device_id=partner, device_id_type=MESH)
    pl.semaphore_wait(barrier, 4)

    def remote(src, dst, sems, target):
        return pltpu.make_async_remote_copy(
            src_ref=src,
            dst_ref=dst,
            send_sem=sems.at[0],
            recv_sem=sems.at[1],
            device_id=target,
            device_id_type=MESH,
        )

    def x_copies(side):
        layer = adjoint.at[:, axial - 1] if side == 0 else adjoint.at[:, 0]
        target = above if side == 0 else below
        return (
            remote(layer, x_in.at[side], x_sems.at[side, 0], target),
            remote(wall, x_wall.at[side], x_sems.at[side, 1], target),
        )

    def a_copies(side):
        target = after if side == 0 else before
        return (
            remote(a_out.at[side], a_in.at[side], a_sems.at[side, 0], target),
            remote(wall, a_wall.at[side], a_sems.at[side, 1], target),
        )

    sends = (ax < n_ax - 1, ax > 0)
    takes = (ax > 0, ax < n_ax - 1)
    for side in range(2):

        @pl.when(sends[side])
        def _():
            for copy in x_copies(side):
                copy.start()

    for side in range(2):
        gathers[side].wait()
        for copy in a_copies(side):
            copy.start()

    load.start()
    load.wait()

    def split(p, carry):
        high, low = pieces(matrices[p].T)
        at = pl.multiple_of(p * vertices, vertices)
        pieces_out[:vertices, pl.ds(at, vertices)] = high.astype(BF16)
        pieces_out[vertices:, pl.ds(at, vertices)] = low.astype(BF16)
        return carry

    lax.fori_loop(0, patches, split, 0, unroll=4)

    lane = lax.broadcasted_iota(jnp.int32, (axial, radial), 1)
    for side, (target, at) in enumerate(((a_low, sector - 1), (a_high, 0))):
        for copy in a_copies(side):
            copy.wait()
        fluid = lane >= a_wall[side][:, at : at + 1]
        for c in range(3):
            target[c] = jnp.where(fluid, a_in[side, c], 0.0)

    lane = lax.broadcasted_iota(jnp.int32, (sector, radial), 1).astype(F32)
    for side, (target, at) in enumerate(((x_low, axial - 1), (x_high, 0))):

        @pl.when(sends[side])
        def _():
            for copy in x_copies(side):
                copy.wait_send()

        @pl.when(takes[side])
        def _():
            for copy in x_copies(side):
                copy.wait_recv()
            fluid = lane >= column_of(x_wall[side][at : at + 1, :].astype(F32))
            for c in range(3):
                target[c] = jnp.where(fluid, x_in[side, c], 0.0)

        @pl.when(jnp.logical_not(takes[side]))
        def _():
            target[...] = jnp.zeros(target.shape, F32)


def halos(adjoint, wall, laplacian):
    n_ax, n_az = lax.axis_size("ax"), lax.axis_size("az")
    comps, axial, sector, radial = adjoint.shape
    patches, vertices = laplacian.shape[1:3]
    vmem = pl.BlockSpec(memory_space=pltpu.VMEM)
    anywhere = pl.BlockSpec(memory_space=pl.ANY)
    dma = pltpu.SemaphoreType.DMA
    x_layer = (comps, sector, radial)
    a_layer = (comps, axial, radial)
    return pl.pallas_call(
        functools.partial(halo_kernel, n_ax, n_az),
        out_shape=(
            jax.ShapeDtypeStruct(x_layer, F32),
            jax.ShapeDtypeStruct(x_layer, F32),
            jax.ShapeDtypeStruct(a_layer, F32),
            jax.ShapeDtypeStruct(a_layer, F32),
            jax.ShapeDtypeStruct((2 * vertices, patches * vertices), BF16),
        ),
        in_specs=[anywhere, vmem, anywhere],
        out_specs=(vmem,) * 5,
        scratch_shapes=[
            pltpu.VMEM((2,) + x_layer, F32),
            pltpu.VMEM((2,) + a_layer, F32),
            pltpu.VMEM((2,) + a_layer, F32),
            pltpu.VMEM((2,) + wall.shape, jnp.int32),
            pltpu.VMEM((2,) + wall.shape, jnp.int32),
            pltpu.VMEM(laplacian.shape[1:], F32),
            dma,
            dma((2,)),
            dma((2, 2, 2)),
            dma((2, 2, 2)),
        ],
        compiler_params=pltpu.CompilerParams(
            collective_id=1, has_side_effects=True, vmem_limit_bytes=60 * 2**20
        ),
        name="halos",
    )(adjoint, wall, laplacian)


def shards(adjoint, primal, wall, owner, adjacency, counts, laplacian):
    vertices = laplacian.shape[2]
    *layers, matrices = halos(adjoint, wall, laplacian)
    updated, tiles = stencil(adjoint, primal, wall, layers, vertices)
    tiles = tiles.reshape(-1, 2 * vertices)
    return updated, smooth(tiles, owner, adjacency, counts, matrices, vertices)


def solution(mesh):
    in_specs = (
        P(None, "ax", "az", None),
        P(None, "ax", "az", None),
        P("ax", "az"),
        P("ax", "az"),
        P("ax", "az", None),
        P("ax", "az"),
        P("ax", "az", None, None),
    )
    out_specs = (P(None, "ax", "az", None), P("ax", "az", None))
    return jax.shard_map(shards, mesh=mesh, in_specs=in_specs, out_specs=out_specs, check_vma=False)
```
